512 devices in a mesh: doc: 512 (over y, x, z, core).
Axes of the slice: x: 4, y: 4, z: 16, core: 2. Of those that a mesh axis runs over, the one named last changes fastest.
Arguments:
- documents: bfloat16 [393216, 1024], P('doc'), may hold values from -64 to 64
- labels: bfloat16 [393216, 128], P('doc'), may hold values from -16 to 16
- skeleton: bfloat16 [131072, 1024], P('doc'), may hold values from -64 to 64
- transfer: float32 [2, 4, 256, 256], replicated, may hold values from 0 to 1.5, as said below
- near_peer: int32 [512, 2], P('doc'), may hold values from 0 to 1
- near_live: int32 [512, 2], P('doc'), may hold values 0 or 1
- couple_peer: int32 [512, 3, 2], P('doc'), may hold values from 0 to 1
- couple_live: int32 [512, 3, 2], P('doc'), may hold values 0 or 1
Outputs:
- scores: float32 [393216, 128], P('doc')
The draws below stay inside these ranges and needn't reach their ends.
Inputs may be any that keep to these rules, and one draw needn't show every extreme that they name: `transfer`: entries are not negative.
All inputs are finite; a program needn't handle non-finite values. No bound on the sum of `near_live` or of `couple_live` on one device may be relied on, other than what follows from the above.
Results may differ from the reference program's by a relative error of at most 0.003.
Values may be sent and summed in bfloat16 or wider, within the bound.
A program may use at most 64 MiB of HBM per device.

```python
import math
import jax
import jax.numpy as jnp
from jax import lax

D = 1024
C = 128
R = 256
LEV = 2
SLOTS = 2
DOC_DEV = 768
DOCS = 393216
POINTS = 131072
N_DOC = 512


center_count = 8


center_weight = 0.26


def cluster_centers(key):
    return jnp.clip(jax.random.normal(jax.random.fold_in(key, 5), (center_count, D), jnp.float32), -4.0, 4.0)


def block_mix(key):
    first_key, second_key = jax.random.split(jax.random.fold_in(key, 7))
    block_total = DOCS // DOC_DEV
    first_cluster = jax.random.randint(first_key, (block_total,), 0, center_count)
    second_cluster = (first_cluster + jax.random.randint(second_key, (block_total,), 1, center_count)) % center_count
    return (first_cluster, second_cluster)


def row_clusters(key, salt, row_count, rows_per_block):
    choose_key, any_key = jax.random.split(jax.random.fold_in(key, salt))
    pick_value = jax.random.randint(choose_key, (row_count,), 0, 4)
    anywhere = jax.random.randint(any_key, (row_count,), 0, center_count)
    block_place = jnp.arange(row_count, dtype=jnp.int32) // rows_per_block
    first_cluster, second_cluster = block_mix(key)
    return jnp.where(pick_value < 2, first_cluster[block_place], jnp.where(pick_value == 2, second_cluster[block_place], anywhere))


def spread_rows(key, salt, row_count, rows_per_block, col_count):
    first_key, second_key = jax.random.split(jax.random.fold_in(key, salt), 2)
    centers = cluster_centers(key)
    clusters = row_clusters(key, salt + 100, row_count, rows_per_block)
    base_values = jnp.clip(jax.random.normal(first_key, (row_count, col_count), jnp.float32), -6.0, 6.0)
    base_values = base_values + center_weight * centers[clusters]
    row_scale = jnp.exp(jax.random.uniform(second_key, (row_count, 1), jnp.float32, 0.0, math.log(10.0)))
    return jnp.clip(base_values * row_scale, -64.0, 64.0)


def draw_documents(key, part):
    return spread_rows(key, 11, DOCS, DOC_DEV, D).astype(jnp.bfloat16)


def draw_skeleton(key, part):
    return spread_rows(key, 23, POINTS, R, D).astype(jnp.bfloat16)


def draw_labels(key, part):
    base_key = jax.random.fold_in(key, 47)
    noise_key = jax.random.fold_in(base_key, 0)
    ampl_key = jax.random.fold_in(base_key, 1)
    wave_key = jax.random.fold_in(base_key, 2)
    phase_key = jax.random.fold_in(base_key, 3)
    offset_key = jax.random.fold_in(base_key, 5)
    block_place = (jnp.arange(DOCS, dtype=jnp.int32) // DOC_DEV).astype(jnp.float32)
    amplitudes = 1.5 * jax.random.normal(ampl_key, (3, C), jnp.float32)
    wavelengths = jnp.exp(jax.random.uniform(wave_key, (3, C), jnp.float32, math.log(16.0), math.log(64.0)))
    phases = jax.random.uniform(phase_key, (3, C), jnp.float32, -math.pi, math.pi)
    smooth_part = jnp.zeros((DOCS, C), jnp.float32)
    for term_index in range(3):
        angle_now = 2.0 * math.pi * block_place[:, None] / wavelengths[term_index][None, :] + phases[term_index][None, :]
        smooth_part = smooth_part + amplitudes[term_index][None, :] * jnp.cos(angle_now)
    cluster_offsets = jax.random.uniform(offset_key, (center_count, C), jnp.float32, -8.0, 8.0)
    doc_clusters = row_clusters(key, 111, DOCS, DOC_DEV)
    smooth_part = smooth_part + cluster_offsets[doc_clusters]
    noise_part = jnp.clip(3.0 * jax.random.normal(noise_key, (DOCS, C), jnp.float32), -15.0, 15.0)
    return jnp.clip(noise_part + smooth_part, -16.0, 16.0).astype(jnp.bfloat16)


def draw_transfer(key, part):
    first_key, second_key = jax.random.split(jax.random.fold_in(key, 37))
    diag_values = jnp.exp(jax.random.uniform(first_key, (LEV, 4, R), jnp.float32, math.log(0.5), math.log(1.5)))
    spread_values = jax.random.uniform(second_key, (LEV, 4, R, R), jnp.float32, 0.0, 0.6 / R)
    eye_mask = jnp.eye(R, dtype=jnp.float32)
    return spread_values * (1.0 - eye_mask) + diag_values[:, :, :, None] * eye_mask


def touch_ends(drawn, own_key, least, largest):
    longest = drawn.shape.index(max(drawn.shape))
    spots = []
    for shift in (0, 1):
        where = [jax.random.randint(jax.random.fold_in(own_key, axis), (), 0, length) for axis, length in enumerate(drawn.shape)]
        where[longest] = (where[longest] + shift) % drawn.shape[longest]
        spots.append(tuple(where))
    return drawn.at[spots[0]].set(least).at[spots[1]].set(largest)


def setup_inputs(seed: int = 0) -> dict:
    splits = jax.random.split(jax.random.key(seed), 9)
    documents = draw_documents(jax.random.fold_in(splits[8], 71), 0)
    labels = draw_labels(jax.random.fold_in(splits[8], 71), 0)
    skeleton = draw_skeleton(jax.random.fold_in(splits[8], 71), 0)
    transfer = draw_transfer(jax.random.fold_in(splits[8], 71), 0)
    near_peer = touch_ends(jax.random.randint(splits[4], (N_DOC, SLOTS), 0, 2), jax.random.fold_in(splits[4], 1), 0, 1).astype(jnp.int32)
    near_live = touch_ends((jax.random.randint(splits[5], (N_DOC, SLOTS), 0, 4) < 3).astype(jnp.int32), jax.random.fold_in(splits[5], 1), 0, 1)
    couple_peer = touch_ends(jax.random.randint(splits[6], (N_DOC, LEV + 1, SLOTS), 0, 2), jax.random.fold_in(splits[6], 1), 0, 1).astype(jnp.int32)
    couple_live = touch_ends((jax.random.randint(splits[7], (N_DOC, LEV + 1, SLOTS), 0, 4) < 3).astype(jnp.int32), jax.random.fold_in(splits[7], 1), 0, 1)
    return {"documents": documents, "labels": labels, "skeleton": skeleton, "transfer": transfer, "near_peer": near_peer, "near_live": near_live, "couple_peer": couple_peer, "couple_live": couple_live}


eps_value = 1e-06
far_gain = 64.0
contract_cols = (((1,), (1,)), ((), ()))

def normalize(row_block):
    widened = row_block.astype(jnp.float32)
    inv_scale = lax.rsqrt(lax.optimization_barrier(jnp.mean(widened * widened, axis=-1, keepdims=True)) + eps_value)
    return (widened * inv_scale).astype(jnp.bfloat16)

def square_sums(row_block):
    widened = row_block.astype(jnp.float32)
    return lax.optimization_barrier(jnp.sum(widened * widened, axis=1))

def kernel_tile(left_rows, left_sq, right_rows, right_sq):
    cross_dot = lax.dot_general(left_rows, right_rows, contract_cols, preferred_element_type=jnp.float32)
    feature_width = left_rows.shape[1]
    exponent = (2.0 * feature_width - (left_sq[:, None] + right_sq[None, :] - 2.0 * cross_dot)) / (2.0 * math.sqrt(feature_width))
    return jnp.exp(exponent)

def side_counts(peer_codes, live_flags):
    before_count = lax.optimization_barrier(jnp.sum(live_flags * (peer_codes == 0).astype(jnp.int32), axis=-1))
    after_count = lax.optimization_barrier(jnp.sum(live_flags * (peer_codes == 1).astype(jnp.int32), axis=-1))
    return (before_count, after_count)

def reference(documents, labels, skeleton, transfer, near_peer, near_live, couple_peer, couple_live):
    highest = lax.Precision.HIGHEST
    block_count = N_DOC
    docs_flat = normalize(documents)
    docs_norm = docs_flat.reshape(block_count, DOC_DEV, D)
    docs_sq = square_sums(docs_flat).reshape(block_count, DOC_DEV)
    label_blocks = labels.reshape(block_count, DOC_DEV, C)
    points_flat = normalize(skeleton)
    points_norm = points_flat.reshape(block_count, R, D)
    points_sq = square_sums(points_flat).reshape(block_count, R)
    block_ids = jnp.arange(block_count, dtype=jnp.int32)
    near_before, near_after = side_counts(near_peer, near_live)
    near_before = near_before * (block_ids >= 1).astype(jnp.int32)
    near_after = near_after * (block_ids <= block_count - 2).astype(jnp.int32)
    diagonal = jnp.arange(DOC_DEV)[:, None] == jnp.arange(DOC_DEV)[None, :]

    def near_block(block_id):
        mine_rows = docs_norm[block_id]
        mine_sq = docs_sq[block_id]
        own_tile = jnp.where(diagonal, 0.0, kernel_tile(mine_rows, mine_sq, mine_rows, mine_sq)).astype(jnp.bfloat16)
        near_num = jnp.dot(own_tile, label_blocks[block_id], preferred_element_type=jnp.float32)
        near_den = lax.optimization_barrier(jnp.sum(own_tile.astype(jnp.float32), axis=1))
        partners = (jnp.maximum(block_id - 1, 0), jnp.minimum(block_id + 1, block_count - 1))
        tallies = (near_before[block_id], near_after[block_id])
        for partner, tally_count in zip(partners, tallies):
            pair_tile = kernel_tile(mine_rows, mine_sq, docs_norm[partner], docs_sq[partner]).astype(jnp.bfloat16)
            weight = tally_count.astype(jnp.float32)
            near_num = near_num + weight * jnp.dot(pair_tile, label_blocks[partner], preferred_element_type=jnp.float32)
            near_den = near_den + weight * lax.optimization_barrier(jnp.sum(pair_tile.astype(jnp.float32), axis=1))
        leaf_kernel = kernel_tile(mine_rows, mine_sq, points_norm[block_id], points_sq[block_id]).astype(jnp.bfloat16)
        return (near_num, near_den, leaf_kernel)
    near_num, near_den, leaf_kernel = lax.map(near_block, block_ids)
    kernel_wide = leaf_kernel.astype(jnp.float32)
    leaf_num = jnp.einsum('bir,bic->brc', kernel_wide, label_blocks.astype(jnp.float32), precision=highest) / DOC_DEV
    leaf_den = lax.optimization_barrier(jnp.sum(kernel_wide, axis=1)) / DOC_DEV
    tier_weights = [(leaf_num, leaf_den)]
    node_num, node_den = (leaf_num, leaf_den)
    for height in range(1, LEV + 1):
        grouped_num = node_num.reshape(-1, 4, R, C)
        grouped_den = node_den.reshape(-1, 4, R)
        lifted_num = 0.25 * jnp.einsum('crs,kcrm->kcsm', transfer[height - 1], grouped_num, precision=highest)
        lifted_den = 0.25 * jnp.einsum('crs,kcr->kcs', transfer[height - 1], grouped_den, precision=highest)
        node_num = lifted_num[:, 0] + lifted_num[:, 1] + (lifted_num[:, 2] + lifted_num[:, 3])
        node_den = lifted_den[:, 0] + lifted_den[:, 1] + (lifted_den[:, 2] + lifted_den[:, 3])
        tier_weights.append((node_num, node_den))
    couple_before, couple_after = side_counts(couple_peer, couple_live)
    couplings = []
    for height in range(LEV + 1):
        stride = 4 ** height
        sent_num = tier_weights[height][0].astype(jnp.bfloat16)
        sent_den = tier_weights[height][1].astype(jnp.bfloat16)
        before_tally = couple_before[:, height] * (block_ids >= stride).astype(jnp.int32)
        after_tally = couple_after[:, height] * (block_ids <= block_count - 1 - stride).astype(jnp.int32)

        def couple_block(block_id):
            total_num = jnp.zeros((R, C), jnp.float32)
            total_den = jnp.zeros((R,), jnp.float32)
            partners = (jnp.maximum(block_id - stride, 0), jnp.minimum(block_id + stride, block_count - 1))
            tallies = (before_tally[block_id], after_tally[block_id])
            for partner, tally_count in zip(partners, tallies):
                pair_kernel = kernel_tile(points_norm[block_id], points_sq[block_id], points_norm[partner], points_sq[partner]).astype(jnp.bfloat16)
                node_id = partner // stride
                weight = tally_count.astype(jnp.float32)
                total_num = total_num + weight * jnp.dot(pair_kernel, sent_num[node_id], preferred_element_type=jnp.float32)
                total_den = total_den + weight * jnp.dot(pair_kernel, sent_den[node_id], preferred_element_type=jnp.float32)
            return (total_num / R, total_den / R)
        couplings.append(lax.map(couple_block, block_ids))
    down_num, down_den = couplings[LEV]
    for height in range(LEV, 0, -1):
        child_slot = block_ids // 4 ** (height - 1) % 4
        transfer_mat = transfer[height - 1][child_slot]
        down_num = couplings[height - 1][0] + jnp.einsum('brs,bsc->brc', transfer_mat, down_num, precision=highest)
        down_den = couplings[height - 1][1] + jnp.einsum('brs,bs->br', transfer_mat, down_den, precision=highest)
    far_num = far_gain / R * jnp.einsum('bir,brc->bic', kernel_wide, down_num, precision=highest)
    far_den = far_gain / R * jnp.einsum('bir,br->bi', kernel_wide, down_den, precision=highest)
    scores = (near_num + far_num) / (near_den + far_den)[:, :, None]
    return scores.reshape(block_count * DOC_DEV, C)
```

```python
import functools
import math

import jax
import jax.numpy as jnp
from jax import lax
from jax.experimental import pallas as pl
from jax.experimental.pallas import tpu as pltpu
from jax.sharding import PartitionSpec as P

MESH = pl.DeviceIdType.MESH
f32 = jnp.float32
bf16 = jnp.bfloat16
highest = lax.Precision.HIGHEST
eps_value = 1e-06
far_gain = 64.0
chunk = 256
aug = 144

PTS_UP8, PTS_DOWN8, PTS_UP2, PTS_DOWN2, PTS_DOWN1 = range(5)
DOCS = 5
LABELS = 8
W0 = 9
T1 = 10
T2 = 13
W1, W2 = 16, 17
RET0 = 18
RET1_DOWN, RET1_UP, RET2_DOWN, RET2_UP = 19, 20, 21, 22
NEAR = 23
FLOWS = 26


def dot_nn(a, b, precision=None):
    return lax.dot_general(
        a, b, (((1,), (0,)), ((), ())), precision=precision, preferred_element_type=f32
    )


def dot_nt(a, b, precision=None):
    return lax.dot_general(
        a, b, (((1,), (1,)), ((), ())), precision=precision, preferred_element_type=f32
    )


def normalize(rows):
    wide = rows.astype(f32)
    scale = lax.rsqrt(jnp.mean(wide * wide, axis=-1, keepdims=True) + eps_value)
    return (wide * scale).astype(bf16)


def bias_of(rows):
    wide = rows.astype(f32)
    width = rows.shape[1]
    return (width - jnp.sum(wide * wide, axis=1, keepdims=True)) / (2.0 * math.sqrt(width))


def as_row(column):
    return jnp.broadcast_to(column, (column.shape[0], 128)).T[0:1, :]


def kernel_tile(left, left_bias, right, right_bias_row):
    cross = dot_nt(left, right)
    return jnp.exp(cross * (1.0 / math.sqrt(left.shape[1])) + (left_bias + right_bias_row))


def augmented(labels):
    rows = labels.shape[0]
    turned = labels.astype(f32).T
    ones = (lax.broadcasted_iota(jnp.int32, (aug - labels.shape[1], rows), 0) == 0).astype(f32)
    return jnp.concatenate([turned, ones], axis=0).astype(bf16)


def kernel(
    n,
    docs_in,
    labels_in,
    skel_in,
    transfer_in,
    near_peer,
    near_live,
    couple_peer,
    couple_live,
    out_ref,
    docs,
    docs_bias,
    docs_row,
    lab_t,
    pts,
    leaf,
    docs_r,
    labels_r,
    lab_tr,
    p8,
    p2,
    p1,
    near_t,
    before_t,
    w0_send,
    w0_recv,
    t1_send,
    t1_recv,
    t2_send,
    t2_recv,
    w1_own,
    w1_recv,
    w2_own,
    w2_recv,
    ret0_send,
    ret0_recv,
    ret1_send,
    ret1_recv,
    ret2_send,
    ret2_recv,
    near_send,
    near_recv,
    send_sem,
    recv_sem,
):
    me = lax.axis_index("doc")
    count = docs_in.shape[0]
    rank = skel_in.shape[0]
    pieces = count // chunk

    def at(offset):
        return lax.rem(me + offset + n, n)

    def sibling(bits, unit):
        low = lax.rem(me // unit, 2)
        high = lax.rem(me // (2 * unit), 2)
        step = (1 - 2 * low) * (bits % 2) + (2 - 4 * high) * (bits // 2)
        return me + step * unit

    def send(flow, src, dst, target):
        copy = pltpu.make_async_remote_copy(
            src_ref=src,
            dst_ref=dst,
            send_sem=send_sem.at[flow],
            recv_sem=recv_sem.at[flow],
            device_id=(target,),
            device_id_type=MESH,
        )
        copy.start()
        return copy

    low1 = lax.rem(me, 4) < 2
    low2 = lax.rem(me, 16) < 8
    shift1 = jnp.where(low1, at(-2), at(2))
    shift2 = jnp.where(low2, at(-8), at(8))

    barrier = pltpu.get_barrier_semaphore()
    greeted = [at(1), at(-1), at(2), at(-2), at(8), at(-8)]
    greeted += [sibling(3, 1), sibling(1, 4), sibling(3, 4)]
    for other in greeted:
        pl.semaphore_signal(barrier, inc=1, device_id=(other,), device_id_type=MESH)

    pts[...] = normalize(skel_in[...])
    pl.semaphore_wait(barrier, len(greeted))

    c_up8 = send(PTS_UP8, pts, p8.at[0], at(8))
    c_down8 = send(PTS_DOWN8, pts, p8.at[1], at(-8))
    c_up2 = send(PTS_UP2, pts, p2.at[0], at(2))
    c_down2 = send(PTS_DOWN2, pts, p2.at[1], at(-2))
    c_down1 = send(PTS_DOWN1, pts, p1, at(-1))

    def docs_copy(i):
        rows = pl.ds(pl.multiple_of(i * chunk, chunk), chunk)
        return pltpu.make_async_remote_copy(
            src_ref=docs.at[rows],
            dst_ref=docs_r.at[rows],
            send_sem=send_sem.at[DOCS + i],
            recv_sem=recv_sem.at[DOCS + i],
            device_id=(at(1),),
            device_id_type=MESH,
        )

    def near_copy(i):
        return pltpu.make_async_remote_copy(
            src_ref=near_send.at[i],
            dst_ref=near_recv.at[i],
            send_sem=send_sem.at[NEAR + i],
            recv_sem=recv_sem.at[NEAR + i],
            device_id=(at(-1),),
            device_id_type=MESH,
        )

    c_labels = send(LABELS, labels_in, labels_r, at(1))

    @pl.loop(0, pieces)
    def _(i):
        rows = pl.ds(pl.multiple_of(i * chunk, chunk), chunk)
        docs[rows, :] = normalize(docs_in[rows, :])
        docs_copy(i).start()

    lab_t[...] = augmented(labels_in[...])
    pts_bias = bias_of(pts[...])
    pts_row = as_row(pts_bias)

    @pl.loop(0, pieces)
    def _(i):
        rows = pl.ds(pl.multiple_of(i * chunk, chunk), chunk)
        block = docs[rows, :]
        bias = bias_of(block)
        docs_bias[rows, :] = bias
        docs_row[:, rows] = as_row(bias)
        leaf[rows, :] = kernel_tile(block, bias, pts[...], pts_row).astype(bf16)

    w0 = dot_nn(lab_t[...], leaf[...]) * (1.0 / count)
    w0_send[...] = w0.astype(bf16)
    c_w0 = send(W0, w0_send, w0_recv, at(-1))
    child1 = lax.rem(me, 4)
    child2 = lax.rem(me // 4, 4)
    t1 = 0.25 * dot_nn(w0, transfer_in[0, child1], highest)
    t1_send[...] = t1.astype(bf16)
    c_t1 = [send(T1 + j, t1_send, t1_recv.at[j], sibling(j + 1, 1)) for j in range(3)]

    near_t[...] = jnp.zeros_like(near_t)

    @pl.loop(0, pieces)
    def _(i):
        rows = pl.ds(pl.multiple_of(i * chunk, chunk), chunk)
        tile = kernel_tile(docs[rows, :], docs_bias[rows, :], docs[...], docs_row[...])
        row_ids = lax.broadcasted_iota(jnp.int32, tile.shape, 0) + i * chunk
        col_ids = lax.broadcasted_iota(jnp.int32, tile.shape, 1)
        tile = jnp.where(row_ids == col_ids, 0.0, tile).astype(bf16)
        near_t[...] += dot_nn(lab_t[:, rows], tile)

    for copy in c_t1:
        copy.wait_recv()
    w1 = t1 + t1_recv[0].astype(f32) + (t1_recv[1].astype(f32) + t1_recv[2].astype(f32))
    w1_own[...] = w1.astype(bf16)
    c_w1 = send(W1, w1_own, w1_recv, shift1)
    t2 = 0.25 * dot_nn(w1, transfer_in[1, child2], highest)
    t2_send[...] = t2.astype(bf16)
    c_t2 = [send(T2 + j, t2_send, t2_recv.at[j], sibling(j + 1, 4)) for j in range(3)]

    c_down1.wait_recv()
    c_w0.wait_recv()
    pair = kernel_tile(pts[...], pts_bias, p1[...], as_row(bias_of(p1[...]))).astype(bf16)
    ret0_send[...] = dot_nn(w0_send[...], pair).astype(bf16)
    c_ret0 = send(RET0, ret0_send, ret0_recv, at(1))
    after0 = dot_nt(w0_recv[...], pair)

    for copy in c_t2:
        copy.wait_recv()
    w2 = t2 + t2_recv[0].astype(f32) + (t2_recv[1].astype(f32) + t2_recv[2].astype(f32))
    w2_own[...] = w2.astype(bf16)
    c_w2 = send(W2, w2_own, w2_recv, shift2)

    c_up2.wait_recv()
    c_down2.wait_recv()
    c_w1.wait_recv()
    pair = kernel_tile(
        p2[0], bias_of(p2[0]), p2[1], as_row(bias_of(p2[1]))
    ).astype(bf16)
    w_before = jnp.where(low1, w1_recv[...], w1_own[...])
    w_after = jnp.where(low1, w1_own[...], w1_recv[...])
    ret1_send[0] = dot_nt(w_after, pair).astype(bf16)
    ret1_send[1] = dot_nn(w_before, pair).astype(bf16)
    c_ret1 = [
        send(RET1_DOWN, ret1_send.at[0], ret1_recv.at[0], at(-2)),
        send(RET1_UP, ret1_send.at[1], ret1_recv.at[1], at(2)),
    ]

    c_labels.wait_recv()
    lab_tr[...] = augmented(labels_r[...])
    before_t[...] = jnp.zeros_like(before_t)

    @pl.loop(0, pieces)
    def _(i):
        rows = pl.ds(pl.multiple_of(i * chunk, chunk), chunk)
        docs_copy(i).wait_recv()
        block = docs_r[rows, :]
        tile = kernel_tile(block, bias_of(block), docs[...], docs_row[...]).astype(bf16)
        near_send[i] = dot_nt(lab_t[...], tile).astype(bf16)
        near_copy(i).start()
        before_t[...] += dot_nn(lab_tr[:, rows], tile)

    c_up8.wait_recv()
    c_down8.wait_recv()
    c_w2.wait_recv()
    pair = kernel_tile(
        p8[0], bias_of(p8[0]), p8[1], as_row(bias_of(p8[1]))
    ).astype(bf16)
    w_before = jnp.where(low2, w2_recv[...], w2_own[...])
    w_after = jnp.where(low2, w2_own[...], w2_recv[...])
    ret2_send[0] = dot_nt(w_after, pair).astype(bf16)
    ret2_send[1] = dot_nn(w_before, pair).astype(bf16)
    c_ret2 = [
        send(RET2_DOWN, ret2_send.at[0], ret2_recv.at[0], at(-8)),
        send(RET2_UP, ret2_send.at[1], ret2_recv.at[1], at(8)),
    ]

    def tally(peer, live, code, inside):
        total = jnp.int32(0)
        for p, v in zip(peer, live):
            total = total + v * (p == code).astype(jnp.int32)
        return (total * inside.astype(jnp.int32)).astype(f32)

    def tallies(peer, live, stride):
        return (
            tally(peer, live, 0, me >= stride),
            tally(peer, live, 1, me <= n - 1 - stride),
        )

    slots = near_peer.shape[1]
    near_before, near_after = tallies(
        [near_peer[0, j] for j in range(slots)], [near_live[0, j] for j in range(slots)], 1
    )
    couple = [
        tallies(
            [couple_peer[0, level, j] for j in range(slots)],
            [couple_live[0, level, j] for j in range(slots)],
            4**level,
        )
        for level in range(3)
    ]

    c_ret0.wait_recv()
    far0 = (couple[0][0] * ret0_recv[...].astype(f32) + couple[0][1] * after0) / rank
    for copy in c_ret1:
        copy.wait_recv()
    far1 = (
        couple[1][1] * ret1_recv[0].astype(f32) + couple[1][0] * ret1_recv[1].astype(f32)
    ) / rank

    @pl.loop(0, pieces)
    def _(i):
        rows = pl.ds(pl.multiple_of(i * chunk, chunk), chunk)
        near_copy(i).wait_recv()
        near_t[:, rows] += (
            near_before * before_t[:, rows] + near_after * near_recv[i].astype(f32)
        )

    for copy in c_ret2:
        copy.wait_recv()
    down = (
        couple[2][1] * ret2_recv[0].astype(f32) + couple[2][0] * ret2_recv[1].astype(f32)
    ) / rank
    down = far1 + dot_nt(down, transfer_in[1, child2], highest)
    down = far0 + dot_nt(down, transfer_in[0, child1], highest)
    down_high = down.astype(bf16)
    down_low = (down - down_high.astype(f32)).astype(bf16)
    far = dot_nt(down_high, leaf[...]) + dot_nt(down_low, leaf[...])
    total = near_t[...] + (far_gain / rank) * far
    width = labels_in.shape[1]
    out_ref[...] = (total[:width] / total[width : width + 1]).T

    for copy in [c_up8, c_down8, c_up2, c_down2, c_down1, c_labels, c_w0, c_w1, c_w2, c_ret0]:
        copy.wait_send()
    for copy in c_t1 + c_t2 + c_ret1 + c_ret2:
        copy.wait_send()

    @pl.loop(0, pieces)
    def _(i):
        docs_copy(i).wait_send()
        near_copy(i).wait_send()


def solution(mesh):
    n = mesh.shape["doc"]

    def local(documents, labels, skeleton, transfer, near_peer, near_live, couple_peer, couple_live):
        count, depth = documents.shape
        width = labels.shape[1]
        rank = skeleton.shape[0]
        pieces = count // chunk
        node = lambda *lead: pltpu.VMEM((*lead, aug, rank), bf16)
        vmem = pl.BlockSpec(memory_space=pltpu.VMEM)
        smem = pl.BlockSpec(memory_space=pltpu.SMEM)
        return pl.pallas_call(
            functools.partial(kernel, n),
            out_shape=jax.ShapeDtypeStruct((count, width), f32),
            in_specs=[vmem] * 4 + [smem] * 4,
            out_specs=vmem,
            scratch_shapes=[
                pltpu.VMEM((count, depth), bf16),
                pltpu.VMEM((count, 1), f32),
                pltpu.VMEM((1, count), f32),
                pltpu.VMEM((aug, count), bf16),
                pltpu.VMEM((rank, depth), bf16),
                pltpu.VMEM((count, rank), bf16),
                pltpu.VMEM((count, depth), bf16),
                pltpu.VMEM((count, width), bf16),
                pltpu.VMEM((aug, count), bf16),
                pltpu.VMEM((2, rank, depth), bf16),
                pltpu.VMEM((2, rank, depth), bf16),
                pltpu.VMEM((rank, depth), bf16),
                pltpu.VMEM((aug, count), f32),
                pltpu.VMEM((aug, count), f32),
                node(),
                node(),
                node(),
                node(3),
                node(),
                node(3),
                node(),
                node(),
                node(),
                node(),
                node(),
                node(),
                node(2),
                node(2),
                node(2),
                node(2),
                node(pieces),
                node(pieces),
                pltpu.SemaphoreType.DMA((FLOWS,)),
                pltpu.SemaphoreType.DMA((FLOWS,)),
            ],
            compiler_params=pltpu.CompilerParams(
                collective_id=0, has_side_effects=True, vmem_limit_bytes=48 * 2**20
            ),
        )(documents, labels, skeleton, transfer, near_peer, near_live, couple_peer, couple_live)

    placed = (
        P("doc", None),
        P("doc", None),
        P("doc", None),
        P(),
        P("doc", None),
        P("doc", None),
        P("doc", None, None),
        P("doc", None, None),
    )
    return jax.shard_map(
        local, mesh=mesh, in_specs=placed, out_specs=P("doc", None), check_vma=False
    )
```

```python
import functools
import math

import jax
import jax.numpy as jnp
from jax import lax
from jax.experimental import pallas as pl
from jax.experimental.pallas import tpu as pltpu
from jax.sharding import PartitionSpec as P

MESH = pl.DeviceIdType.MESH
f32 = jnp.float32
bf16 = jnp.bfloat16
highest = lax.Precision.HIGHEST
eps_value = 1e-06
far_gain = 64.0
chunk = 256
aug = 144

PTS_UP8, PTS_DOWN8, PTS_UP2, PTS_DOWN, PTS_DOWN1 = range(5)
DOCS = 5
LABELS = 8
W0 = 9
T1 = 10
SHARE1 = 13
W1 = 16
T2 = 17
SHARE2 = 20
SHIFT2 = 23
SHARE_NEXT = 24
RET0 = 27
RET1_DOWN, RET1_UP, RET2_DOWN, RET2_UP = 28, 29, 30, 31
NEAR = 32
FLOWS = 35

part = 48
step_rows = 32

IN_SKEL = 0
IN_LABELS = 1
IN_TRANSFER = 2
IN_LISTS = 3
IN_DOCS = 7
INPUTS = 10


def dot_nn(a, b, precision=None):
    return lax.dot_general(
        a, b, (((1,), (0,)), ((), ())), precision=precision, preferred_element_type=f32
    )


def dot_nt(a, b, precision=None):
    return lax.dot_general(
        a, b, (((1,), (1,)), ((), ())), precision=precision, preferred_element_type=f32
    )


def normalize(rows):
    wide = rows.astype(f32)
    scale = lax.rsqrt(jnp.mean(wide * wide, axis=-1, keepdims=True) + eps_value)
    return (wide * scale).astype(bf16)


def bias_of(rows):
    wide = rows.astype(f32)
    width = rows.shape[1]
    return (width - jnp.sum(wide * wide, axis=1, keepdims=True)) / (2.0 * math.sqrt(width))


def as_row(column):
    return jnp.broadcast_to(column, (column.shape[0], 128)).T[0:1, :]


def kernel_tile(left, left_bias, right, right_bias_row):
    cross = dot_nt(left, right)
    return jnp.exp(cross * (1.0 / math.sqrt(left.shape[1])) + (left_bias + right_bias_row))


def augmented(labels):
    rows = labels.shape[0]
    turned = labels.astype(f32).T
    ones = (lax.broadcasted_iota(jnp.int32, (aug - labels.shape[1], rows), 0) == 0).astype(f32)
    return jnp.concatenate([turned, ones], axis=0).astype(bf16)


def whole(parts):
    last = parts.shape[0] - 1
    return jnp.concatenate(
        [parts[j, :step_rows] for j in range(last)] + [parts[last]], axis=0
    )


def kernel(
    n,
    docs_hbm,
    labels_hbm,
    skel_hbm,
    transfer_hbm,
    near_peer_hbm,
    near_live_hbm,
    couple_peer_hbm,
    couple_live_hbm,
    out_ref,
    docs_in,
    labels_in,
    skel_in,
    transfer_in,
    near_peer,
    near_live,
    couple_peer,
    couple_live,
    docs,
    docs_bias,
    docs_row,
    lab_t,
    pts,
    leaf,
    docs_r,
    labels_r,
    lab_tr,
    p8,
    p2,
    p1,
    near_t,
    before_t,
    w0_send,
    w0_recv,
    t1_sum,
    t1_send,
    t1_recv,
    w1_parts,
    w1_own,
    w1_next,
    t2_send,
    t2_recv,
    w2_parts,
    w2_next,
    ret0_send,
    ret0_recv,
    ret1_send,
    ret1_recv,
    ret2_send,
    ret2_recv,
    near_send,
    near_recv,
    in_sem,
    send_sem,
    recv_sem,
):
    me = lax.axis_index("doc")
    count = docs_in.shape[0]
    rank = skel_in.shape[0]
    pieces = count // chunk
    core = lax.rem(me, 2)
    quarter = lax.rem(me, 4)

    def piece(i):
        return pl.ds(pl.multiple_of(i * chunk, chunk), chunk)

    def part_rows(j):
        return pl.ds(pl.multiple_of(j * step_rows, step_rows), part)

    def fetch(slot, src, dst):
        return pltpu.make_async_copy(src, dst, in_sem.at[slot])

    def docs_fetch(i):
        return fetch(IN_DOCS + i, docs_hbm.at[piece(i)], docs_in.at[piece(i)])

    f_skel = fetch(IN_SKEL, skel_hbm, skel_in)
    f_skel.start()
    for i in range(pieces):
        docs_fetch(i).start()
    f_labels = fetch(IN_LABELS, labels_hbm, labels_in)
    f_labels.start()
    f_transfer = fetch(IN_TRANSFER, transfer_hbm, transfer_in)
    f_transfer.start()
    f_lists = [
        fetch(IN_LISTS, near_peer_hbm, near_peer),
        fetch(IN_LISTS + 1, near_live_hbm, near_live),
        fetch(IN_LISTS + 2, couple_peer_hbm, couple_peer),
        fetch(IN_LISTS + 3, couple_live_hbm, couple_live),
    ]
    for f in f_lists:
        f.start()

    def at(offset):
        return lax.rem(me + offset + n, n)

    def flipped(place, bits):
        low = lax.rem(place, 2)
        high = lax.rem(place // 2, 2)
        return (1 - 2 * low) * (bits % 2) + (2 - 4 * high) * (bits // 2)

    def sibling(bits, unit):
        return me + flipped(me // unit, bits) * unit

    def send(flow, src, dst, target):
        copy = pltpu.make_async_remote_copy(
            src_ref=src,
            dst_ref=dst,
            send_sem=send_sem.at[flow],
            recv_sem=recv_sem.at[flow],
            device_id=(target,),
            device_id_type=MESH,
        )
        copy.start()
        return copy

    even = core == 0
    odd = core == 1
    next1 = jnp.where(even, jnp.where(quarter < 2, at(-2), at(2)), at(-4))
    low1 = jnp.logical_and(even, quarter < 2)
    low2 = lax.rem(me, 16) < 8
    next2 = jnp.where(low2, at(-8), at(8))

    barrier = pltpu.get_barrier_semaphore()
    greeted = [at(1), at(-1), at(2), at(-2), at(4), at(-4), at(8), at(-8)]
    greeted += [sibling(3, 1), sibling(3, 4)]
    for other in greeted:
        pl.semaphore_signal(barrier, inc=1, device_id=(other,), device_id_type=MESH)

    f_skel.wait()
    pts[...] = normalize(skel_in[...])
    pl.semaphore_wait(barrier, len(greeted))

    c_up8 = send(PTS_UP8, pts, p8.at[0], at(8))
    c_down8 = send(PTS_DOWN8, pts, p8.at[1], at(-8))

    def up2_copy():
        return pltpu.make_async_remote_copy(
            src_ref=pts,
            dst_ref=p2.at[0],
            send_sem=send_sem.at[PTS_UP2],
            recv_sem=recv_sem.at[PTS_UP2],
            device_id=(at(2),),
            device_id_type=MESH,
        )

    def ret1_down_copy():
        return pltpu.make_async_remote_copy(
            src_ref=ret1_send.at[0],
            dst_ref=ret1_recv.at[0],
            send_sem=send_sem.at[RET1_DOWN],
            recv_sem=recv_sem.at[RET1_DOWN],
            device_id=(at(-2),),
            device_id_type=MESH,
        )

    c_down = send(PTS_DOWN, pts, p2.at[1], jnp.where(even, at(-2), at(-4)))

    @pl.when(even)
    def _():
        up2_copy().start()

    c_down1 = send(PTS_DOWN1, pts, p1, at(-1))

    def docs_copy(i):
        return pltpu.make_async_remote_copy(
            src_ref=docs.at[piece(i)],
            dst_ref=docs_r.at[piece(i)],
            send_sem=send_sem.at[DOCS + i],
            recv_sem=recv_sem.at[DOCS + i],
            device_id=(at(1),),
            device_id_type=MESH,
        )

    def near_copy(i):
        return pltpu.make_async_remote_copy(
            src_ref=near_send.at[i],
            dst_ref=near_recv.at[i],
            send_sem=send_sem.at[NEAR + i],
            recv_sem=recv_sem.at[NEAR + i],
            device_id=(at(-1),),
            device_id_type=MESH,
        )

    @pl.loop(0, pieces)
    def _(i):
        docs_fetch(i).wait()
        docs[piece(i), :] = normalize(docs_in[piece(i), :])
        docs_copy(i).start()

    f_labels.wait()
    c_labels = send(LABELS, labels_in, labels_r, at(1))
    lab_t[...] = augmented(labels_in[...])
    pts_bias = bias_of(pts[...])
    pts_row = as_row(pts_bias)

    @pl.loop(0, pieces)
    def _(i):
        rows = piece(i)
        block = docs[rows, :]
        bias = bias_of(block)
        docs_bias[rows, :] = bias
        docs_row[:, rows] = as_row(bias)
        leaf[rows, :] = kernel_tile(block, bias, pts[...], pts_row).astype(bf16)

    w0 = dot_nn(lab_t[...], leaf[...]) * (1.0 / count)
    w0_send[...] = w0.astype(bf16)
    c_w0 = send(W0, w0_send, w0_recv, at(-1))

    f_transfer.wait()
    child2 = lax.rem(me // 4, 4)
    t1 = 0.25 * dot_nn(w0, transfer_in[0, quarter], highest)
    t1_sum[...] = t1
    t1_send[...] = t1.astype(bf16)
    c_t1 = [
        send(
            T1 + j,
            t1_send.at[part_rows(quarter + flipped(quarter, j + 1))],
            t1_recv.at[j],
            sibling(j + 1, 1),
        )
        for j in range(3)
    ]

    near_t[...] = jnp.zeros_like(near_t)

    @pl.loop(0, pieces)
    def _(i):
        rows = piece(i)
        tile = kernel_tile(docs[rows, :], docs_bias[rows, :], docs[...], docs_row[...])
        row_ids = lax.broadcasted_iota(jnp.int32, tile.shape, 0) + i * chunk
        col_ids = lax.broadcasted_iota(jnp.int32, tile.shape, 1)
        tile = jnp.where(row_ids == col_ids, 0.0, tile).astype(bf16)
        near_t[...] += dot_nn(lab_t[:, rows], tile)

    for copy in c_t1:
        copy.wait_recv()
    w1 = (t1_sum[part_rows(quarter), :] + t1_recv[0].astype(f32)) + (
        t1_recv[1].astype(f32) + t1_recv[2].astype(f32)
    )
    w1_parts[quarter] = w1.astype(bf16)
    c_share1 = [
        send(SHARE1 + j, w1_parts.at[quarter], w1_parts.at[quarter], sibling(j + 1, 1))
        for j in range(3)
    ]
    t2 = 0.25 * dot_nn(w1, transfer_in[1, child2], highest)
    t2_send[...] = t2.astype(bf16)
    c_t2 = [send(T2 + j, t2_send, t2_recv.at[j], sibling(j + 1, 4)) for j in range(3)]

    c_down1.wait_recv()
    c_w0.wait_recv()
    pair = kernel_tile(pts[...], pts_bias, p1[...], as_row(bias_of(p1[...]))).astype(bf16)
    ret0_send[...] = dot_nn(w0_send[...], pair).astype(bf16)
    c_ret0 = send(RET0, ret0_send, ret0_recv, at(1))
    after0 = dot_nt(w0_recv[...], pair)

    for copy in c_t2:
        copy.wait_recv()
    w2 = (t2 + t2_recv[0].astype(f32)) + (t2_recv[1].astype(f32) + t2_recv[2].astype(f32))
    w2_parts[quarter] = w2.astype(bf16)
    c_shift2 = send(SHIFT2, w2_parts.at[quarter], w2_next.at[quarter], next2)
    c_share2 = [
        send(SHARE2 + j, w2_parts.at[quarter], w2_parts.at[quarter], sibling(j + 1, 1))
        for j in range(3)
    ]

    for copy in c_share1:
        copy.wait_recv()
    w1_own[...] = whole(w1_parts)
    c_w1 = send(W1, w1_own, w1_next, next1)

    c_shift2.wait_recv()
    c_share_next = [
        send(SHARE_NEXT + j, w2_next.at[quarter], w2_next.at[quarter], sibling(j + 1, 1))
        for j in range(3)
    ]

    c_down.wait_recv()

    @pl.when(even)
    def _():
        up2_copy().wait_recv()

    @pl.when(odd)
    def _():
        p2[0] = pts[...]

    c_w1.wait_recv()
    pair = kernel_tile(
        p2[0], bias_of(p2[0]), p2[1], as_row(bias_of(p2[1]))
    ).astype(bf16)
    w_before = jnp.where(low1, w1_next[...], w1_own[...])
    w_after = jnp.where(low1, w1_own[...], w1_next[...])
    ret1_send[0] = dot_nt(w_after, pair).astype(bf16)
    ret1_send[1] = dot_nn(w_before, pair).astype(bf16)
    c_ret1 = send(
        RET1_UP, ret1_send.at[1], ret1_recv.at[1], jnp.where(even, at(2), at(4))
    )

    @pl.when(even)
    def _():
        ret1_down_copy().start()

    @pl.when(odd)
    def _():
        ret1_recv[0] = ret1_send[0]

    c_labels.wait_recv()
    lab_tr[...] = augmented(labels_r[...])
    before_t[...] = jnp.zeros_like(before_t)

    @pl.loop(0, pieces)
    def _(i):
        rows = piece(i)
        docs_copy(i).wait_recv()
        block = docs_r[rows, :]
        tile = kernel_tile(block, bias_of(block), docs[...], docs_row[...]).astype(bf16)
        near_send[i] = dot_nt(lab_t[...], tile).astype(bf16)
        near_copy(i).start()
        before_t[...] += dot_nn(lab_tr[:, rows], tile)

    for copy in c_share2 + c_share_next:
        copy.wait_recv()
    own2 = whole(w2_parts)
    other2 = whole(w2_next)
    w_before = jnp.where(low2, other2, own2)
    w_after = jnp.where(low2, own2, other2)
    c_up8.wait_recv()
    c_down8.wait_recv()
    pair = kernel_tile(
        p8[0], bias_of(p8[0]), p8[1], as_row(bias_of(p8[1]))
    ).astype(bf16)
    ret2_send[0] = dot_nt(w_after, pair).astype(bf16)
    ret2_send[1] = dot_nn(w_before, pair).astype(bf16)
    c_ret2 = [
        send(RET2_DOWN, ret2_send.at[0], ret2_recv.at[0], at(-8)),
        send(RET2_UP, ret2_send.at[1], ret2_recv.at[1], at(8)),
    ]

    def tally(peer, live, code, inside):
        total = jnp.int32(0)
        for p, v in zip(peer, live):
            total = total + v * (p == code).astype(jnp.int32)
        return (total * inside.astype(jnp.int32)).astype(f32)

    def tallies(peer, live, stride):
        return (
            tally(peer, live, 0, me >= stride),
            tally(peer, live, 1, me <= n - 1 - stride),
        )

    for f in f_lists:
        f.wait()
    slots = near_peer.shape[1]
    near_before, near_after = tallies(
        [near_peer[0, j] for j in range(slots)], [near_live[0, j] for j in range(slots)], 1
    )
    couple = [
        tallies(
            [couple_peer[0, j, level] for j in range(slots)],
            [couple_live[0, j, level] for j in range(slots)],
            4**level,
        )
        for level in range(3)
    ]

    c_ret0.wait_recv()
    far0 = (couple[0][0] * ret0_recv[...].astype(f32) + couple[0][1] * after0) / rank
    c_ret1.wait_recv()

    @pl.when(even)
    def _():
        ret1_down_copy().wait_recv()

    far1 = (
        couple[1][1] * ret1_recv[0].astype(f32) + couple[1][0] * ret1_recv[1].astype(f32)
    ) / rank

    @pl.loop(0, pieces)
    def _(i):
        rows = piece(i)
        near_copy(i).wait_recv()
        near_t[:, rows] += (
            near_before * before_t[:, rows] + near_after * near_recv[i].astype(f32)
        )

    for copy in c_ret2:
        copy.wait_recv()
    down = (
        couple[2][1] * ret2_recv[0].astype(f32) + couple[2][0] * ret2_recv[1].astype(f32)
    ) / rank
    down = far1 + dot_nt(down, transfer_in[1, child2], highest)
    down = far0 + dot_nt(down, transfer_in[0, quarter], highest)
    down_high = down.astype(bf16)
    down_low = (down - down_high.astype(f32)).astype(bf16)
    far = dot_nt(down_high, leaf[...]) + dot_nt(down_low, leaf[...])
    total = near_t[...] + (far_gain / rank) * far
    width = labels_in.shape[1]
    out_ref[...] = (total[:width] / total[width : width + 1]).T

    sent = [c_up8, c_down8, c_down, c_down1, c_labels, c_w0, c_w1, c_shift2, c_ret0, c_ret1]
    for copy in sent + c_t1 + c_share1 + c_t2 + c_share2 + c_share_next + c_ret2:
        copy.wait_send()

    @pl.when(even)
    def _():
        up2_copy().wait_send()
        ret1_down_copy().wait_send()

    @pl.loop(0, pieces)
    def _(i):
        docs_copy(i).wait_send()
        near_copy(i).wait_send()


def solution(mesh):
    n = mesh.shape["doc"]

    def local(documents, labels, skeleton, transfer, near_peer, near_live, couple_peer, couple_live):
        count, depth = documents.shape
        width = labels.shape[1]
        rank = skeleton.shape[0]
        pieces = count // chunk
        node = lambda *lead: pltpu.VMEM((*lead, aug, rank), bf16)
        parts = lambda lead: pltpu.VMEM((lead, part, rank), bf16)
        anywhere = pl.BlockSpec(memory_space=pl.ANY)
        couple_peer = couple_peer.transpose(0, 2, 1)
        couple_live = couple_live.transpose(0, 2, 1)
        return pl.pallas_call(
            functools.partial(kernel, n),
            out_shape=jax.ShapeDtypeStruct((count, width), f32),
            in_specs=[anywhere] * 8,
            out_specs=pl.BlockSpec(memory_space=pltpu.VMEM),
            scratch_shapes=[
                pltpu.VMEM((count, depth), bf16),
                pltpu.VMEM((count, width), bf16),
                pltpu.VMEM((rank, depth), bf16),
                pltpu.VMEM(transfer.shape, f32),
                pltpu.SMEM(near_peer.shape, jnp.int32),
                pltpu.SMEM(near_live.shape, jnp.int32),
                pltpu.SMEM(couple_peer.shape, jnp.int32),
                pltpu.SMEM(couple_live.shape, jnp.int32),
                pltpu.VMEM((count, depth), bf16),
                pltpu.VMEM((count, 1), f32),
                pltpu.VMEM((1, count), f32),
                pltpu.VMEM((aug, count), bf16),
                pltpu.VMEM((rank, depth), bf16),
                pltpu.VMEM((count, rank), bf16),
                pltpu.VMEM((count, depth), bf16),
                pltpu.VMEM((count, width), bf16),
                pltpu.VMEM((aug, count), bf16),
                pltpu.VMEM((2, rank, depth), bf16),
                pltpu.VMEM((2, rank, depth), bf16),
                pltpu.VMEM((rank, depth), bf16),
                pltpu.VMEM((aug, count), f32),
                pltpu.VMEM((aug, count), f32),
                node(),
                node(),
                pltpu.VMEM((aug, rank), f32),
                node(),
                parts(3),
                parts(4),
                node(),
                node(),
                pltpu.VMEM((part, rank), bf16),
                parts(3),
                parts(4),
                parts(4),
                node(),
                node(),
                node(2),
                node(2),
                node(2),
                node(2),
                node(pieces),
                node(pieces),
                pltpu.SemaphoreType.DMA((INPUTS,)),
                pltpu.SemaphoreType.DMA((FLOWS,)),
                pltpu.SemaphoreType.DMA((FLOWS,)),
            ],
            compiler_params=pltpu.CompilerParams(
                collective_id=0, has_side_effects=True, vmem_limit_bytes=60 * 2**20
            ),
        )(documents, labels, skeleton, transfer, near_peer, near_live, couple_peer, couple_live)

    placed = (
        P("doc", None),
        P("doc", None),
        P("doc", None),
        P(),
        P("doc", None),
        P("doc", None),
        P("doc", None, None),
        P("doc", None, None),
    )
    return jax.shard_map(
        local, mesh=mesh, in_specs=placed, out_specs=P("doc", None), check_vma=False
    )
```

```python
import functools
import math

import jax
import jax.numpy as jnp
from jax import lax
from jax.experimental import pallas as pl
from jax.experimental.pallas import tpu as pltpu
from jax.sharding import PartitionSpec as P

MESH = pl.DeviceIdType.MESH
f32 = jnp.float32
bf16 = jnp.bfloat16
highest = lax.Precision.HIGHEST
eps_value = 1e-06
far_gain = 64.0
chunk = 256
aug = 144

PTS_UP2, PTS_DOWN, PTS_DOWN1 = range(3)
DOCS = 5
LABELS = 8
W0 = 9
T1 = 10
SHARE1 = 13
W1 = 16
T2 = 17
SHARE2 = 20
SHIFT2 = 23
SHARE_NEXT = 24
RET0 = 27
RET1_DOWN, RET1_UP, RET2_DOWN, RET2_UP = 28, 29, 30, 31
NEAR = 32
PTS_UP8, PTS_DOWN8 = 35, 39
FLOWS = 43

strips = 4

part = 48
step_rows = 32

IN_SKEL = 0
IN_LABELS = 1
IN_TRANSFER = 2
IN_LISTS = 3
IN_DOCS = 7
INPUTS = 10


def dot_nn(a, b, precision=None):
    return lax.dot_general(
        a, b, (((1,), (0,)), ((), ())), precision=precision, preferred_element_type=f32
    )


def dot_nt(a, b, precision=None):
    return lax.dot_general(
        a, b, (((1,), (1,)), ((), ())), precision=precision, preferred_element_type=f32
    )


def normalize(rows):
    wide = rows.astype(f32)
    scale = lax.rsqrt(jnp.mean(wide * wide, axis=-1, keepdims=True) + eps_value)
    return (wide * scale).astype(bf16)


def bias_of(rows):
    wide = rows.astype(f32)
    width = rows.shape[1]
    return (width - jnp.sum(wide * wide, axis=1, keepdims=True)) / (2.0 * math.sqrt(width))


def as_row(column):
    return jnp.broadcast_to(column, (column.shape[0], 128)).T[0:1, :]


def kernel_tile(left, left_bias, right, right_bias_row):
    cross = dot_nt(left, right)
    return jnp.exp(cross * (1.0 / math.sqrt(left.shape[1])) + (left_bias + right_bias_row))


def augmented(labels):
    rows = labels.shape[0]
    turned = labels.astype(f32).T
    ones = (lax.broadcasted_iota(jnp.int32, (aug - labels.shape[1], rows), 0) == 0).astype(f32)
    return jnp.concatenate([turned, ones], axis=0).astype(bf16)


def whole(parts):
    last = parts.shape[0] - 1
    return jnp.concatenate(
        [parts[j, :step_rows] for j in range(last)] + [parts[last]], axis=0
    )


def kernel(
    n,
    docs_hbm,
    labels_hbm,
    skel_hbm,
    transfer_hbm,
    near_peer_hbm,
    near_live_hbm,
    couple_peer_hbm,
    couple_live_hbm,
    out_ref,
    docs_in,
    labels_in,
    skel_in,
    transfer_in,
    near_peer,
    near_live,
    couple_peer,
    couple_live,
    docs,
    docs_bias,
    docs_row,
    lab_t,
    pts,
    leaf,
    docs_r,
    labels_r,
    lab_tr,
    p8,
    p2,
    p1,
    near_t,
    before_t,
    w0_send,
    w0_recv,
    t1_sum,
    t1_send,
    t1_recv,
    w1_parts,
    w1_own,
    w1_next,
    t2_send,
    t2_recv,
    w2_parts,
    w2_next,
    ret0_send,
    ret0_recv,
    ret1_send,
    ret1_recv,
    ret2_send,
    ret2_recv,
    near_send,
    near_recv,
    in_sem,
    send_sem,
    recv_sem,
):
    me = lax.axis_index("doc")
    count = docs_in.shape[0]
    rank = skel_in.shape[0]
    pieces = count // chunk
    core = lax.rem(me, 2)
    quarter = lax.rem(me, 4)

    def piece(i):
        return pl.ds(pl.multiple_of(i * chunk, chunk), chunk)

    def part_rows(j):
        return pl.ds(pl.multiple_of(j * step_rows, step_rows), part)

    def fetch(slot, src, dst):
        return pltpu.make_async_copy(src, dst, in_sem.at[slot])

    def docs_fetch(i):
        return fetch(IN_DOCS + i, docs_hbm.at[piece(i)], docs_in.at[piece(i)])

    f_skel = fetch(IN_SKEL, skel_hbm, skel_in)
    f_skel.start()
    for i in range(pieces):
        docs_fetch(i).start()
    f_labels = fetch(IN_LABELS, labels_hbm, labels_in)
    f_labels.start()
    f_transfer = fetch(IN_TRANSFER, transfer_hbm, transfer_in)
    f_transfer.start()
    f_lists = [
        fetch(IN_LISTS, near_peer_hbm, near_peer),
        fetch(IN_LISTS + 1, near_live_hbm, near_live),
        fetch(IN_LISTS + 2, couple_peer_hbm, couple_peer),
        fetch(IN_LISTS + 3, couple_live_hbm, couple_live),
    ]
    for f in f_lists:
        f.start()

    def at(offset):
        return lax.rem(me + offset + n, n)

    def flipped(place, bits):
        low = lax.rem(place, 2)
        high = lax.rem(place // 2, 2)
        return (1 - 2 * low) * (bits % 2) + (2 - 4 * high) * (bits // 2)

    def sibling(bits, unit):
        return me + flipped(me // unit, bits) * unit

    def send(flow, src, dst, target):
        copy = pltpu.make_async_remote_copy(
            src_ref=src,
            dst_ref=dst,
            send_sem=send_sem.at[flow],
            recv_sem=recv_sem.at[flow],
            device_id=(target,),
            device_id_type=MESH,
        )
        copy.start()
        return copy

    even = core == 0
    odd = core == 1
    next1 = jnp.where(even, jnp.where(quarter < 2, at(-2), at(2)), at(-4))
    low1 = jnp.logical_and(even, quarter < 2)
    low2 = lax.rem(me, 16) < 8
    next2 = jnp.where(low2, at(-8), at(8))

    barrier = pltpu.get_barrier_semaphore()
    greeted = [at(1), at(-1), at(2), at(-2), at(4), at(-4), at(8), at(-8)]
    greeted += [sibling(3, 1), sibling(3, 4)]
    for other in greeted:
        pl.semaphore_signal(barrier, inc=1, device_id=(other,), device_id_type=MESH)

    f_skel.wait()
    pts[...] = normalize(skel_in[...])
    pl.semaphore_wait(barrier, len(greeted))

    def strip_copy(slot, k):
        size = rank // strips
        rows = pl.ds(k * size, size)
        return pltpu.make_async_remote_copy(
            src_ref=pts.at[rows],
            dst_ref=p8.at[slot, rows],
            send_sem=send_sem.at[(PTS_UP8, PTS_DOWN8)[slot] + k],
            recv_sem=recv_sem.at[(PTS_UP8, PTS_DOWN8)[slot] + k],
            device_id=(at((8, -8)[slot]),),
            device_id_type=MESH,
        )

    def strip(k):
        strip_copy(0, k).start()
        strip_copy(1, k).start()

    strip(0)

    def up2_copy():
        return pltpu.make_async_remote_copy(
            src_ref=pts,
            dst_ref=p2.at[0],
            send_sem=send_sem.at[PTS_UP2],
            recv_sem=recv_sem.at[PTS_UP2],
            device_id=(at(2),),
            device_id_type=MESH,
        )

    def ret1_down_copy():
        return pltpu.make_async_remote_copy(
            src_ref=ret1_send.at[0],
            dst_ref=ret1_recv.at[0],
            send_sem=send_sem.at[RET1_DOWN],
            recv_sem=recv_sem.at[RET1_DOWN],
            device_id=(at(-2),),
            device_id_type=MESH,
        )

    def docs_copy(i):
        return pltpu.make_async_remote_copy(
            src_ref=docs.at[piece(i)],
            dst_ref=docs_r.at[piece(i)],
            send_sem=send_sem.at[DOCS + i],
            recv_sem=recv_sem.at[DOCS + i],
            device_id=(at(1),),
            device_id_type=MESH,
        )

    def near_copy(i):
        return pltpu.make_async_remote_copy(
            src_ref=near_send.at[i],
            dst_ref=near_recv.at[i],
            send_sem=send_sem.at[NEAR + i],
            recv_sem=recv_sem.at[NEAR + i],
            device_id=(at(-1),),
            device_id_type=MESH,
        )

    @pl.loop(0, pieces)
    def _(i):
        docs_fetch(i).wait()
        docs[piece(i), :] = normalize(docs_in[piece(i), :])

    f_labels.wait()
    lab_t[...] = augmented(labels_in[...])
    pts_bias = bias_of(pts[...])
    pts_row = as_row(pts_bias)

    @pl.loop(0, pieces)
    def _(i):
        rows = piece(i)
        block = docs[rows, :]
        bias = bias_of(block)
        docs_bias[rows, :] = bias
        docs_row[:, rows] = as_row(bias)
        leaf[rows, :] = kernel_tile(block, bias, pts[...], pts_row).astype(bf16)

    w0 = dot_nn(lab_t[...], leaf[...]) * (1.0 / count)
    w0_send[...] = w0.astype(bf16)

    f_transfer.wait()
    child2 = lax.rem(me // 4, 4)
    t1 = 0.25 * dot_nn(w0, transfer_in[0, quarter], highest)
    t1_sum[...] = t1
    t1_send[...] = t1.astype(bf16)
    c_t1 = [
        send(
            T1 + j,
            t1_send.at[part_rows(quarter + flipped(quarter, j + 1))],
            t1_recv.at[j],
            sibling(j + 1, 1),
        )
        for j in range(3)
    ]

    c_w0 = send(W0, w0_send, w0_recv, at(-1))
    strip(1)

    near_t[...] = jnp.zeros_like(near_t)

    @pl.loop(0, pieces)
    def _(i):
        rows = piece(i)
        tile = kernel_tile(docs[rows, :], docs_bias[rows, :], docs[...], docs_row[...])
        row_ids = lax.broadcasted_iota(jnp.int32, tile.shape, 0) + i * chunk
        col_ids = lax.broadcasted_iota(jnp.int32, tile.shape, 1)
        tile = jnp.where(row_ids == col_ids, 0.0, tile).astype(bf16)
        near_t[...] += dot_nn(lab_t[:, rows], tile)

    for copy in c_t1:
        copy.wait_recv()
    w1 = (t1_sum[part_rows(quarter), :] + t1_recv[0].astype(f32)) + (
        t1_recv[1].astype(f32) + t1_recv[2].astype(f32)
    )
    w1_parts[quarter] = w1.astype(bf16)
    t2 = 0.25 * dot_nn(w1, transfer_in[1, child2], highest)
    t2_send[...] = t2.astype(bf16)
    c_t2 = [send(T2 + j, t2_send, t2_recv.at[j], sibling(j + 1, 4)) for j in range(3)]
    c_share1 = [
        send(SHARE1 + j, w1_parts.at[quarter], w1_parts.at[quarter], sibling(j + 1, 1))
        for j in range(3)
    ]
    strip(2)

    for copy in c_t2:
        copy.wait_recv()
    w2 = (t2 + t2_recv[0].astype(f32)) + (t2_recv[1].astype(f32) + t2_recv[2].astype(f32))
    w2_parts[quarter] = w2.astype(bf16)
    c_shift2 = send(SHIFT2, w2_parts.at[quarter], w2_next.at[quarter], next2)
    c_share2 = [
        send(SHARE2 + j, w2_parts.at[quarter], w2_parts.at[quarter], sibling(j + 1, 1))
        for j in range(3)
    ]

    for copy in c_share1:
        copy.wait_recv()
    w1_own[...] = whole(w1_parts)
    c_w1 = send(W1, w1_own, w1_next, next1)
    strip(3)

    c_shift2.wait_recv()
    c_share_next = [
        send(SHARE_NEXT + j, w2_next.at[quarter], w2_next.at[quarter], sibling(j + 1, 1))
        for j in range(3)
    ]

    c_down1 = send(PTS_DOWN1, pts, p1, at(-1))
    c_down = send(PTS_DOWN, pts, p2.at[1], jnp.where(even, at(-2), at(-4)))

    @pl.when(even)
    def _():
        up2_copy().start()

    c_labels = send(LABELS, labels_in, labels_r, at(1))
    docs_copy(0).start()

    for copy in c_share2 + c_share_next:
        copy.wait_recv()
    own2 = whole(w2_parts)
    other2 = whole(w2_next)
    w_before = jnp.where(low2, other2, own2)
    w_after = jnp.where(low2, own2, other2)
    for k in range(strips):
        strip_copy(0, k).wait_recv()
        strip_copy(1, k).wait_recv()
    pair = kernel_tile(
        p8[0], bias_of(p8[0]), p8[1], as_row(bias_of(p8[1]))
    ).astype(bf16)
    ret2_send[0] = dot_nt(w_after, pair).astype(bf16)
    ret2_send[1] = dot_nn(w_before, pair).astype(bf16)
    c_ret2 = [
        send(RET2_DOWN, ret2_send.at[0], ret2_recv.at[0], at(-8)),
        send(RET2_UP, ret2_send.at[1], ret2_recv.at[1], at(8)),
    ]

    @pl.loop(1, pieces)
    def _(i):
        docs_copy(i).start()

    c_down1.wait_recv()
    c_w0.wait_recv()
    pair = kernel_tile(pts[...], pts_bias, p1[...], as_row(bias_of(p1[...]))).astype(bf16)
    ret0_send[...] = dot_nn(w0_send[...], pair).astype(bf16)
    c_ret0 = send(RET0, ret0_send, ret0_recv, at(1))
    after0 = dot_nt(w0_recv[...], pair)

    c_down.wait_recv()

    @pl.when(even)
    def _():
        up2_copy().wait_recv()

    @pl.when(odd)
    def _():
        p2[0] = pts[...]

    c_w1.wait_recv()
    pair = kernel_tile(
        p2[0], bias_of(p2[0]), p2[1], as_row(bias_of(p2[1]))
    ).astype(bf16)
    w_before = jnp.where(low1, w1_next[...], w1_own[...])
    w_after = jnp.where(low1, w1_own[...], w1_next[...])
    ret1_send[0] = dot_nt(w_after, pair).astype(bf16)
    ret1_send[1] = dot_nn(w_before, pair).astype(bf16)
    c_ret1 = send(
        RET1_UP, ret1_send.at[1], ret1_recv.at[1], jnp.where(even, at(2), at(4))
    )

    @pl.when(even)
    def _():
        ret1_down_copy().start()

    @pl.when(odd)
    def _():
        ret1_recv[0] = ret1_send[0]

    c_labels.wait_recv()
    lab_tr[...] = augmented(labels_r[...])
    before_t[...] = jnp.zeros_like(before_t)

    @pl.loop(0, pieces)
    def _(i):
        rows = piece(i)
        docs_copy(i).wait_recv()
        block = docs_r[rows, :]
        tile = kernel_tile(block, bias_of(block), docs[...], docs_row[...]).astype(bf16)
        near_send[i] = dot_nt(lab_t[...], tile).astype(bf16)
        near_copy(i).start()
        before_t[...] += dot_nn(lab_tr[:, rows], tile)

    def tally(peer, live, code, inside):
        total = jnp.int32(0)
        for p, v in zip(peer, live):
            total = total + v * (p == code).astype(jnp.int32)
        return (total * inside.astype(jnp.int32)).astype(f32)

    def tallies(peer, live, stride):
        return (
            tally(peer, live, 0, me >= stride),
            tally(peer, live, 1, me <= n - 1 - stride),
        )

    for f in f_lists:
        f.wait()
    slots = near_peer.shape[1]
    near_before, near_after = tallies(
        [near_peer[0, j] for j in range(slots)], [near_live[0, j] for j in range(slots)], 1
    )
    couple = [
        tallies(
            [couple_peer[0, j, level] for j in range(slots)],
            [couple_live[0, j, level] for j in range(slots)],
            4**level,
        )
        for level in range(3)
    ]

    c_ret0.wait_recv()
    far0 = (couple[0][0] * ret0_recv[...].astype(f32) + couple[0][1] * after0) / rank
    c_ret1.wait_recv()

    @pl.when(even)
    def _():
        ret1_down_copy().wait_recv()

    far1 = (
        couple[1][1] * ret1_recv[0].astype(f32) + couple[1][0] * ret1_recv[1].astype(f32)
    ) / rank

    for copy in c_ret2:
        copy.wait_recv()
    down = (
        couple[2][1] * ret2_recv[0].astype(f32) + couple[2][0] * ret2_recv[1].astype(f32)
    ) / rank
    down = far1 + dot_nt(down, transfer_in[1, child2], highest)
    down = far0 + dot_nt(down, transfer_in[0, quarter], highest)
    down_high = down.astype(bf16)
    down_low = (down - down_high.astype(f32)).astype(bf16)
    far = dot_nt(down_high, leaf[...]) + dot_nt(down_low, leaf[...])

    @pl.loop(0, pieces)
    def _(i):
        rows = piece(i)
        near_copy(i).wait_recv()
        near_t[:, rows] += (
            near_before * before_t[:, rows] + near_after * near_recv[i].astype(f32)
        )

    total = near_t[...] + (far_gain / rank) * far
    width = labels_in.shape[1]
    out_ref[...] = (total[:width] / total[width : width + 1]).T

    sent = [c_down, c_down1, c_labels, c_w0, c_w1, c_shift2, c_ret0, c_ret1]
    for copy in sent + c_t1 + c_share1 + c_t2 + c_share2 + c_share_next + c_ret2:
        copy.wait_send()

    for k in range(strips):
        strip_copy(0, k).wait_send()
        strip_copy(1, k).wait_send()

    @pl.when(even)
    def _():
        up2_copy().wait_send()
        ret1_down_copy().wait_send()

    @pl.loop(0, pieces)
    def _(i):
        docs_copy(i).wait_send()
        near_copy(i).wait_send()


def solution(mesh):
    n = mesh.shape["doc"]

    def local(documents, labels, skeleton, transfer, near_peer, near_live, couple_peer, couple_live):
        count, depth = documents.shape
        width = labels.shape[1]
        rank = skeleton.shape[0]
        pieces = count // chunk
        node = lambda *lead: pltpu.VMEM((*lead, aug, rank), bf16)
        parts = lambda lead: pltpu.VMEM((lead, part, rank), bf16)
        anywhere = pl.BlockSpec(memory_space=pl.ANY)
        couple_peer = couple_peer.transpose(0, 2, 1)
        couple_live = couple_live.transpose(0, 2, 1)
        return pl.pallas_call(
            functools.partial(kernel, n),
            out_shape=jax.ShapeDtypeStruct((count, width), f32),
            in_specs=[anywhere] * 8,
            out_specs=pl.BlockSpec(memory_space=pltpu.VMEM),
            scratch_shapes=[
                pltpu.VMEM((count, depth), bf16),
                pltpu.VMEM((count, width), bf16),
                pltpu.VMEM((rank, depth), bf16),
                pltpu.VMEM(transfer.shape, f32),
                pltpu.SMEM(near_peer.shape, jnp.int32),
                pltpu.SMEM(near_live.shape, jnp.int32),
                pltpu.SMEM(couple_peer.shape, jnp.int32),
                pltpu.SMEM(couple_live.shape, jnp.int32),
                pltpu.VMEM((count, depth), bf16),
                pltpu.VMEM((count, 1), f32),
                pltpu.VMEM((1, count), f32),
                pltpu.VMEM((aug, count), bf16),
                pltpu.VMEM((rank, depth), bf16),
                pltpu.VMEM((count, rank), bf16),
                pltpu.VMEM((count, depth), bf16),
                pltpu.VMEM((count, width), bf16),
                pltpu.VMEM((aug, count), bf16),
                pltpu.VMEM((2, rank, depth), bf16),
                pltpu.VMEM((2, rank, depth), bf16),
                pltpu.VMEM((rank, depth), bf16),
                pltpu.VMEM((aug, count), f32),
                pltpu.VMEM((aug, count), f32),
                node(),
                node(),
                pltpu.VMEM((aug, rank), f32),
                node(),
                parts(3),
                parts(4),
                node(),
                node(),
                pltpu.VMEM((part, rank), bf16),
                parts(3),
                parts(4),
                parts(4),
                node(),
                node(),
                node(2),
                node(2),
                node(2),
                node(2),
                node(pieces),
                node(pieces),
                pltpu.SemaphoreType.DMA((INPUTS,)),
                pltpu.SemaphoreType.DMA((FLOWS,)),
                pltpu.SemaphoreType.DMA((FLOWS,)),
            ],
            compiler_params=pltpu.CompilerParams(
                collective_id=0, has_side_effects=True, vmem_limit_bytes=60 * 2**20
            ),
        )(documents, labels, skeleton, transfer, near_peer, near_live, couple_peer, couple_live)

    placed = (
        P("doc", None),
        P("doc", None),
        P("doc", None),
        P(),
        P("doc", None),
        P("doc", None),
        P("doc", None, None),
        P("doc", None, None),
    )
    return jax.shard_map(
        local, mesh=mesh, in_specs=placed, out_specs=P("doc", None), check_vma=False
    )
```

```python
import functools
import math

import jax
import jax.numpy as jnp
from jax import lax
from jax.experimental import pallas as pl
from jax.experimental.pallas import tpu as pltpu
from jax.sharding import PartitionSpec as P

MESH = pl.DeviceIdType.MESH
f32 = jnp.float32
bf16 = jnp.bfloat16
highest = lax.Precision.HIGHEST
eps_value = 1e-06
far_gain = 64.0
chunk = 256
aug = 144

PTS_UP2, PTS_DOWN, PTS_DOWN1 = range(3)
DOCS = 5
LABELS = 8
W0 = 9
T1 = 10
SHARE1 = 13
W1 = 16
T2 = 17
SHARE2 = 20
SHIFT2 = 23
SHARE_NEXT = 24
RET0 = 27
RET1_DOWN, RET1_UP = 28, 29
NEAR = 30
PTS8 = 33
FORWARD, W_FORWARD = 37, 38
RET2 = 39
FLOWS = 43

strips = 2

part = 48
step_rows = 32

IN_SKEL = 0
IN_LABELS = 1
IN_TRANSFER = 2
IN_LISTS = 3
IN_DOCS = 7
INPUTS = 10


def dot_nn(a, b, precision=None):
    return lax.dot_general(
        a, b, (((1,), (0,)), ((), ())), precision=precision, preferred_element_type=f32
    )


def dot_nt(a, b, precision=None):
    return lax.dot_general(
        a, b, (((1,), (1,)), ((), ())), precision=precision, preferred_element_type=f32
    )


def normalize(rows):
    wide = rows.astype(f32)
    scale = lax.rsqrt(jnp.mean(wide * wide, axis=-1, keepdims=True) + eps_value)
    return (wide * scale).astype(bf16)


def bias_of(rows):
    wide = rows.astype(f32)
    width = rows.shape[1]
    return (width - jnp.sum(wide * wide, axis=1, keepdims=True)) / (2.0 * math.sqrt(width))


def as_row(column):
    return jnp.broadcast_to(column, (column.shape[0], 128)).T[0:1, :]


def kernel_tile(left, left_bias, right, right_bias_row):
    cross = dot_nt(left, right)
    return jnp.exp(cross * (1.0 / math.sqrt(left.shape[1])) + (left_bias + right_bias_row))


def augmented(labels):
    rows = labels.shape[0]
    turned = labels.astype(f32).T
    ones = (lax.broadcasted_iota(jnp.int32, (aug - labels.shape[1], rows), 0) == 0).astype(f32)
    return jnp.concatenate([turned, ones], axis=0).astype(bf16)


def whole(parts):
    last = parts.shape[0] - 1
    return jnp.concatenate(
        [parts[j, :step_rows] for j in range(last)] + [parts[last]], axis=0
    )


def kernel(
    n,
    docs_hbm,
    labels_hbm,
    skel_hbm,
    transfer_hbm,
    near_peer_hbm,
    near_live_hbm,
    couple_peer_hbm,
    couple_live_hbm,
    out_ref,
    docs_in,
    labels_in,
    skel_in,
    transfer_in,
    near_peer,
    near_live,
    couple_peer,
    couple_live,
    docs,
    docs_bias,
    docs_row,
    lab_t,
    pts,
    leaf,
    docs_r,
    labels_r,
    lab_tr,
    p8,
    p2,
    p1,
    near_t,
    before_t,
    w0_send,
    w0_recv,
    t1_sum,
    t1_send,
    t1_recv,
    w1_parts,
    w1_own,
    w1_next,
    t2_send,
    t2_recv,
    w2_parts,
    w2_next,
    w2_pair,
    ret0_send,
    ret0_recv,
    ret1_send,
    ret1_recv,
    ret2_send,
    ret2_recv,
    near_send,
    near_recv,
    in_sem,
    send_sem,
    recv_sem,
):
    me = lax.axis_index("doc")
    count = docs_in.shape[0]
    rank = skel_in.shape[0]
    pieces = count // chunk
    core = lax.rem(me, 2)
    quarter = lax.rem(me, 4)

    def piece(i):
        return pl.ds(pl.multiple_of(i * chunk, chunk), chunk)

    def part_rows(j):
        return pl.ds(pl.multiple_of(j * step_rows, step_rows), part)

    def fetch(slot, src, dst):
        return pltpu.make_async_copy(src, dst, in_sem.at[slot])

    def docs_fetch(i):
        return fetch(IN_DOCS + i, docs_hbm.at[piece(i)], docs_in.at[piece(i)])

    f_skel = fetch(IN_SKEL, skel_hbm, skel_in)
    f_skel.start()
    for i in range(pieces):
        docs_fetch(i).start()
    f_labels = fetch(IN_LABELS, labels_hbm, labels_in)
    f_labels.start()
    f_transfer = fetch(IN_TRANSFER, transfer_hbm, transfer_in)
    f_transfer.start()
    f_lists = [
        fetch(IN_LISTS, near_peer_hbm, near_peer),
        fetch(IN_LISTS + 1, near_live_hbm, near_live),
        fetch(IN_LISTS + 2, couple_peer_hbm, couple_peer),
        fetch(IN_LISTS + 3, couple_live_hbm, couple_live),
    ]
    for f in f_lists:
        f.start()

    def at(offset):
        return lax.rem(me + offset + n, n)

    def flipped(place, bits):
        low = lax.rem(place, 2)
        high = lax.rem(place // 2, 2)
        return (1 - 2 * low) * (bits % 2) + (2 - 4 * high) * (bits // 2)

    def sibling(bits, unit):
        return me + flipped(me // unit, bits) * unit

    def inside(offset):
        return jnp.logical_and(me + offset >= 0, me + offset < n)

    class Flow:
        def __init__(self, flow, src, dst, target, out=None, into=None):
            self.copy = pltpu.make_async_remote_copy(
                src_ref=src,
                dst_ref=dst,
                send_sem=send_sem.at[flow],
                recv_sem=recv_sem.at[flow],
                device_id=(target,),
                device_id_type=MESH,
            )
            self.out = out
            self.into = into

        def start(self):
            when(self.out, self.copy.start)
            return self

        def wait_recv(self):
            when(self.into, self.copy.wait_recv)

        def wait_send(self):
            when(self.out, self.copy.wait_send)

    def when(condition, action):
        if condition is None:
            action()
        else:
            pl.when(condition)(lambda: action() and None)

    def along(flow, src, dst, offset, out=True, into=True):
        return Flow(
            flow,
            src,
            dst,
            at(offset),
            inside(offset) if out is True else jnp.logical_and(inside(offset), out),
            inside(-offset) if into is True else jnp.logical_and(inside(-offset), into),
        )

    def send(flow, src, dst, target, out=None, into=None):
        return Flow(flow, src, dst, target, out, into).start()

    even = core == 0
    odd = core == 1
    next1 = jnp.where(even, jnp.where(quarter < 2, at(-2), at(2)), at(-4))
    low1 = jnp.logical_and(even, quarter < 2)

    out1 = jnp.where(even, jnp.where(quarter < 2, me >= 2, me + 2 < n), me >= 4)
    into1 = jnp.where(even, out1, me + 4 < n)

    spot = lax.rem(me // 2, 16)
    base = me - lax.rem(me, 32)
    up4 = base + lax.rem(spot + 4, 16) * 2 + core
    down4 = base + lax.rem(spot + 12, 16) * 2 + core
    half = spot // 8
    central = jnp.logical_and(spot >= 4, spot < 12)
    meet = central == even
    first_half = half == 0
    meeting = jnp.where(first_half == even, up4, down4)
    from_a = jnp.where(even, down4, up4)
    from_b = jnp.where(even, up4, down4)
    other_half = jnp.where(central == first_half, up4, down4)
    has_next = me < n - 32
    has_last = me >= 32
    meet_next = jnp.logical_and(meet, has_next)
    meet_last = jnp.logical_and(meet, has_last)
    b_next = jnp.logical_and(half == 1, has_next)
    a_last = jnp.logical_and(first_half, has_last)

    barrier = pltpu.get_barrier_semaphore()
    reach = (1, 2, 4, 32)
    for other in [sibling(3, 1), sibling(3, 4), up4, down4]:
        pl.semaphore_signal(barrier, inc=1, device_id=(other,), device_id_type=MESH)
    for offset in [sign * far for far in reach for sign in (1, -1)]:

        @pl.when(inside(offset))
        def _(offset=offset):
            pl.semaphore_signal(barrier, inc=1, device_id=(at(offset),), device_id_type=MESH)

    @pl.when(b_next)
    def _():
        pl.semaphore_signal(barrier, inc=1, device_id=(meeting + 32,), device_id_type=MESH)

    @pl.when(jnp.logical_and(first_half, jnp.logical_not(has_last)))
    def _():
        ret2_recv[1] = jnp.zeros_like(ret2_recv[1])

    @pl.when(jnp.logical_and(half == 1, jnp.logical_not(has_next)))
    def _():
        ret2_recv[0] = jnp.zeros_like(ret2_recv[0])

    @pl.when(me < 4)
    def _():
        p2[0] = jnp.zeros_like(p2[0])
        ret1_recv[1] = jnp.zeros_like(ret1_recv[1])

    @pl.when(me >= n - 4)
    def _():
        p2[1] = jnp.zeros_like(p2[1])
        ret1_recv[0] = jnp.zeros_like(ret1_recv[0])

    @pl.when(jnp.logical_not(into1))
    def _():
        w1_next[...] = jnp.zeros_like(w1_next)

    @pl.when(me == 0)
    def _():
        docs_r[...] = jnp.zeros_like(docs_r)
        labels_r[...] = jnp.zeros_like(labels_r)
        ret0_recv[...] = jnp.zeros_like(ret0_recv)

    @pl.when(me == n - 1)
    def _():
        p1[...] = jnp.zeros_like(p1)
        w0_recv[...] = jnp.zeros_like(w0_recv)
        near_recv[...] = jnp.zeros_like(near_recv)

    f_skel.wait()
    pts[...] = normalize(skel_in[...])
    greetings = 4 + jnp.where(meet_last, 1, 0)
    for offset in [sign * far for far in reach for sign in (1, -1)]:
        greetings = greetings + jnp.where(inside(offset), 1, 0)
    pl.semaphore_wait(barrier, greetings)

    def strip_copy(slot, k):
        size = rank // strips
        rows = pl.ds(k * size, size)
        return Flow(
            PTS8 + slot * strips + k, pts.at[rows], p8.at[slot, rows], meeting, None, meet
        )

    def strip(k):
        strip_copy(half, k).start()

    strip(0)

    def docs_copy(i):
        return along(DOCS + i, docs.at[piece(i)], docs_r.at[piece(i)], 1)

    def near_copy(i):
        return along(NEAR + i, near_send.at[i], near_recv.at[i], -1)

    @pl.loop(0, pieces)
    def _(i):
        docs_fetch(i).wait()
        docs[piece(i), :] = normalize(docs_in[piece(i), :])

    f_labels.wait()
    lab_t[...] = augmented(labels_in[...])
    pts_bias = bias_of(pts[...])
    pts_row = as_row(pts_bias)

    @pl.loop(0, pieces)
    def _(i):
        rows = piece(i)
        block = docs[rows, :]
        bias = bias_of(block)
        docs_bias[rows, :] = bias
        docs_row[:, rows] = as_row(bias)
        leaf[rows, :] = kernel_tile(block, bias, pts[...], pts_row).astype(bf16)

    w0 = dot_nn(lab_t[...], leaf[...]) * (1.0 / count)
    w0_send[...] = w0.astype(bf16)

    f_transfer.wait()
    child2 = lax.rem(me // 4, 4)
    t1 = 0.25 * dot_nn(w0, transfer_in[0, quarter], highest)
    t1_sum[...] = t1
    t1_send[...] = t1.astype(bf16)
    c_t1 = [
        send(
            T1 + j,
            t1_send.at[part_rows(quarter + flipped(quarter, j + 1))],
            t1_recv.at[j],
            sibling(j + 1, 1),
        )
        for j in range(3)
    ]

    c_w0 = along(W0, w0_send, w0_recv, -1).start()
    strip(1)

    near_t[...] = jnp.zeros_like(near_t)

    @pl.loop(0, pieces)
    def _(i):
        rows = piece(i)
        tile = kernel_tile(docs[rows, :], docs_bias[rows, :], docs[...], docs_row[...])
        row_ids = lax.broadcasted_iota(jnp.int32, tile.shape, 0) + i * chunk
        col_ids = lax.broadcasted_iota(jnp.int32, tile.shape, 1)
        tile = jnp.where(row_ids == col_ids, 0.0, tile).astype(bf16)
        near_t[...] += dot_nn(lab_t[:, rows], tile)

    for copy in c_t1:
        copy.wait_recv()
    w1 = (t1_sum[part_rows(quarter), :] + t1_recv[0].astype(f32)) + (
        t1_recv[1].astype(f32) + t1_recv[2].astype(f32)
    )
    w1_parts[quarter] = w1.astype(bf16)
    t2 = 0.25 * dot_nn(w1, transfer_in[1, child2], highest)
    t2_send[...] = t2.astype(bf16)
    c_t2 = [send(T2 + j, t2_send, t2_recv.at[j], sibling(j + 1, 4)) for j in range(3)]
    c_share1 = [
        send(SHARE1 + j, w1_parts.at[quarter], w1_parts.at[quarter], sibling(j + 1, 1))
        for j in range(3)
    ]
    level1 = [
        along(PTS_DOWN, pts, p2.at[1], -2, even, even),
        along(PTS_DOWN, pts, p2.at[1], -4, odd, odd),
        along(PTS_UP2, pts, p2.at[0], 2, even, even),
    ]
    for copy in level1:
        copy.start()

    for copy in c_t2:
        copy.wait_recv()
    w2 = (t2 + t2_recv[0].astype(f32)) + (t2_recv[1].astype(f32) + t2_recv[2].astype(f32))
    w2_parts[quarter] = w2.astype(bf16)
    c_shift2 = send(SHIFT2, w2_parts.at[quarter], w2_next.at[quarter], other_half)
    c_share2 = [
        send(
            SHARE2 + j,
            w2_parts.at[quarter],
            w2_parts.at[quarter],
            sibling(j + 1, 1),
            meet if j == 1 else jnp.logical_not(meet),
            meet,
        )
        for j in range(3)
    ]

    for copy in c_share1:
        copy.wait_recv()
    w1_own[...] = whole(w1_parts)
    c_w1 = send(W1, w1_own, w1_next, next1, out1, into1)
    for k in range(strips):
        strip_copy(1, k).wait_recv()
    c_forward = send(FORWARD, p8.at[1], p8.at[2], at(32), meet_next, meet_last)
    c_down1 = along(PTS_DOWN1, pts, p1, -1).start()
    c_labels = along(LABELS, labels_in, labels_r, 1).start()

    c_shift2.wait_recv()
    c_share_next = [
        send(
            SHARE_NEXT + j,
            w2_next.at[quarter],
            w2_next.at[quarter],
            sibling(j + 1, 1),
            meet if j == 1 else jnp.logical_not(meet),
            meet,
        )
        for j in range(3)
    ]

    docs_copy(0).start()

    for copy in c_share2 + c_share_next:
        copy.wait_recv()

    @pl.when(meet)
    def _():
        own2 = whole(w2_parts)
        other2 = whole(w2_next)
        w2_pair[0] = jnp.where(first_half, own2, other2)
        w2_pair[1] = jnp.where(first_half, other2, own2)

    c_wforward = send(W_FORWARD, w2_pair.at[1], w2_pair.at[2], at(32), meet_next, meet_last)
    for k in range(strips):
        strip_copy(0, k).wait_recv()

    def couple2(left, right):
        return kernel_tile(
            left, bias_of(left), right, as_row(bias_of(right))
        ).astype(bf16)

    @pl.when(meet)
    def _():
        pair = couple2(p8[0], p8[1])
        ret2_send[0] = dot_nt(w2_pair[1], pair).astype(bf16)
        ret2_send[1] = dot_nn(w2_pair[0], pair).astype(bf16)

    def ret2(j, slot, target, out, into):
        return send(RET2 + j, ret2_send.at[j], ret2_recv.at[slot], target, out, into)

    c_ret2 = [
        ret2(0, 0, from_a, meet, first_half),
        ret2(1, 1, from_b, meet, half == 1),
    ]
    c_forward.wait_recv()
    c_wforward.wait_recv()

    @pl.when(meet_last)
    def _():
        pair = couple2(p8[2], p8[0])
        ret2_send[2] = dot_nt(w2_pair[0], pair).astype(bf16)
        ret2_send[3] = dot_nn(w2_pair[2], pair).astype(bf16)

    c_ret2 += [
        ret2(2, 0, from_b - 32, meet_last, b_next),
        ret2(3, 1, from_a, meet_last, a_last),
    ]

    @pl.loop(1, pieces)
    def _(i):
        docs_copy(i).start()

    c_down1.wait_recv()
    c_w0.wait_recv()
    pair = kernel_tile(pts[...], pts_bias, p1[...], as_row(bias_of(p1[...]))).astype(bf16)
    ret0_send[...] = dot_nn(w0_send[...], pair).astype(bf16)
    c_ret0 = along(RET0, ret0_send, ret0_recv, 1).start()
    after0 = dot_nt(w0_recv[...], pair)

    for copy in level1:
        copy.wait_recv()

    @pl.when(odd)
    def _():
        p2[0] = pts[...]

    c_w1.wait_recv()
    pair = kernel_tile(
        p2[0], bias_of(p2[0]), p2[1], as_row(bias_of(p2[1]))
    ).astype(bf16)
    w_before = jnp.where(low1, w1_next[...], w1_own[...])
    w_after = jnp.where(low1, w1_own[...], w1_next[...])
    ret1_send[0] = dot_nt(w_after, pair).astype(bf16)
    ret1_send[1] = dot_nn(w_before, pair).astype(bf16)
    c_ret1 = [
        along(RET1_UP, ret1_send.at[1], ret1_recv.at[1], 2, even, even).start(),
        along(RET1_UP, ret1_send.at[1], ret1_recv.at[1], 4, odd, odd).start(),
        along(RET1_DOWN, ret1_send.at[0], ret1_recv.at[0], -2, even, even).start(),
    ]

    @pl.when(odd)
    def _():
        ret1_recv[0] = ret1_send[0]

    c_labels.wait_recv()
    lab_tr[...] = augmented(labels_r[...])
    before_t[...] = jnp.zeros_like(before_t)

    @pl.loop(0, pieces)
    def _(i):
        rows = piece(i)
        docs_copy(i).wait_recv()
        block = docs_r[rows, :]
        tile = kernel_tile(block, bias_of(block), docs[...], docs_row[...]).astype(bf16)
        near_send[i] = dot_nt(lab_t[...], tile).astype(bf16)
        near_copy(i).start()
        before_t[...] += dot_nn(lab_tr[:, rows], tile)

    def tally(peer, live, code, inside):
        total = jnp.int32(0)
        for p, v in zip(peer, live):
            total = total + v * (p == code).astype(jnp.int32)
        return (total * inside.astype(jnp.int32)).astype(f32)

    def tallies(peer, live, stride):
        return (
            tally(peer, live, 0, me >= stride),
            tally(peer, live, 1, me <= n - 1 - stride),
        )

    for f in f_lists:
        f.wait()
    slots = near_peer.shape[1]
    near_before, near_after = tallies(
        [near_peer[0, j] for j in range(slots)], [near_live[0, j] for j in range(slots)], 1
    )
    couple = [
        tallies(
            [couple_peer[0, j, level] for j in range(slots)],
            [couple_live[0, j, level] for j in range(slots)],
            4**level,
        )
        for level in range(3)
    ]

    c_ret0.wait_recv()
    far0 = (couple[0][0] * ret0_recv[...].astype(f32) + couple[0][1] * after0) / rank
    for copy in c_ret1:
        copy.wait_recv()

    far1 = (
        couple[1][1] * ret1_recv[0].astype(f32) + couple[1][0] * ret1_recv[1].astype(f32)
    ) / rank

    for copy in c_ret2:
        copy.wait_recv()
    down = (
        couple[2][1] * ret2_recv[0].astype(f32) + couple[2][0] * ret2_recv[1].astype(f32)
    ) / rank
    down = far1 + dot_nt(down, transfer_in[1, child2], highest)
    down = far0 + dot_nt(down, transfer_in[0, quarter], highest)
    down_high = down.astype(bf16)
    down_low = (down - down_high.astype(f32)).astype(bf16)
    far = dot_nt(down_high, leaf[...]) + dot_nt(down_low, leaf[...])

    @pl.loop(0, pieces)
    def _(i):
        rows = piece(i)
        near_copy(i).wait_recv()
        near_t[:, rows] += (
            near_before * before_t[:, rows] + near_after * near_recv[i].astype(f32)
        )

    total = near_t[...] + (far_gain / rank) * far
    width = labels_in.shape[1]
    out_ref[...] = (total[:width] / total[width : width + 1]).T

    for copies in (
        [c_down1, c_labels, c_w0, c_w1, c_shift2, c_ret0],
        c_t1 + c_share1 + c_t2 + c_share2 + c_share_next,
        level1 + c_ret1 + c_ret2,
        [c_forward, c_wforward] + [strip_copy(half, k) for k in range(strips)],
    ):
        for copy in copies:
            copy.wait_send()

    @pl.loop(0, pieces)
    def _(i):
        docs_copy(i).wait_send()
        near_copy(i).wait_send()


def solution(mesh):
    n = mesh.shape["doc"]

    def local(documents, labels, skeleton, transfer, near_peer, near_live, couple_peer, couple_live):
        count, depth = documents.shape
        width = labels.shape[1]
        rank = skeleton.shape[0]
        pieces = count // chunk
        node = lambda *lead: pltpu.VMEM((*lead, aug, rank), bf16)
        parts = lambda lead: pltpu.VMEM((lead, part, rank), bf16)
        anywhere = pl.BlockSpec(memory_space=pl.ANY)
        couple_peer = couple_peer.transpose(0, 2, 1)
        couple_live = couple_live.transpose(0, 2, 1)
        return pl.pallas_call(
            functools.partial(kernel, n),
            out_shape=jax.ShapeDtypeStruct((count, width), f32),
            in_specs=[anywhere] * 8,
            out_specs=pl.BlockSpec(memory_space=pltpu.VMEM),
            scratch_shapes=[
                pltpu.VMEM((count, depth), bf16),
                pltpu.VMEM((count, width), bf16),
                pltpu.VMEM((rank, depth), bf16),
                pltpu.VMEM(transfer.shape, f32),
                pltpu.SMEM(near_peer.shape, jnp.int32),
                pltpu.SMEM(near_live.shape, jnp.int32),
                pltpu.SMEM(couple_peer.shape, jnp.int32),
                pltpu.SMEM(couple_live.shape, jnp.int32),
                pltpu.VMEM((count, depth), bf16),
                pltpu.VMEM((count, 1), f32),
                pltpu.VMEM((1, count), f32),
                pltpu.VMEM((aug, count), bf16),
                pltpu.VMEM((rank, depth), bf16),
                pltpu.VMEM((count, rank), bf16),
                pltpu.VMEM((count, depth), bf16),
                pltpu.VMEM((count, width), bf16),
                pltpu.VMEM((aug, count), bf16),
                pltpu.VMEM((3, rank, depth), bf16),
                pltpu.VMEM((2, rank, depth), bf16),
                pltpu.VMEM((rank, depth), bf16),
                pltpu.VMEM((aug, count), f32),
                pltpu.VMEM((aug, count), f32),
                node(),
                node(),
                pltpu.VMEM((aug, rank), f32),
                node(),
                parts(3),
                parts(4),
                node(),
                node(),
                pltpu.VMEM((part, rank), bf16),
                parts(3),
                parts(4),
                parts(4),
                node(3),
                node(),
                node(),
                node(2),
                node(2),
                node(4),
                node(2),
                node(pieces),
                node(pieces),
                pltpu.SemaphoreType.DMA((INPUTS,)),
                pltpu.SemaphoreType.DMA((FLOWS,)),
                pltpu.SemaphoreType.DMA((FLOWS,)),
            ],
            compiler_params=pltpu.CompilerParams(
                collective_id=0, has_side_effects=True, vmem_limit_bytes=60 * 2**20
            ),
        )(documents, labels, skeleton, transfer, near_peer, near_live, couple_peer, couple_live)

    placed = (
        P("doc", None),
        P("doc", None),
        P("doc", None),
        P(),
        P("doc", None),
        P("doc", None),
        P("doc", None, None),
        P("doc", None, None),
    )
    return jax.shard_map(
        local, mesh=mesh, in_specs=placed, out_specs=P("doc", None), check_vma=False
    )
```

```python
import functools
import math

import jax
import jax.numpy as jnp
from jax import lax
from jax.experimental import pallas as pl
from jax.experimental.pallas import tpu as pltpu
from jax.sharding import PartitionSpec as P

MESH = pl.DeviceIdType.MESH
f32 = jnp.float32
bf16 = jnp.bfloat16
highest = lax.Precision.HIGHEST
eps_value = 1e-06
far_gain = 64.0
chunk = 256
aug = 144

PTS_UP2, PTS_DOWN, PTS_DOWN1 = range(3)
DOCS = 5
LABELS = 8
W0 = 9
T1 = 10
SHARE1 = 13
W1 = 16
T2 = 17
SHARE2 = 20
SHIFT2 = 23
SHARE_NEXT = 24
RET0 = 27
RET1_DOWN, RET1_UP = 28, 29
NEAR = 30
PTS8 = 33
FORWARD, W_FORWARD = 37, 38
RET2 = 39
FLOWS = 43

strips = 2

part = 48
step_rows = 32

IN_SKEL = 0
IN_LABELS = 1
IN_TRANSFER = 2
IN_LISTS = 3
IN_DOCS = 7
INPUTS = 10


def dot_nn(a, b, precision=None):
    return lax.dot_general(
        a, b, (((1,), (0,)), ((), ())), precision=precision, preferred_element_type=f32
    )


def dot_nt(a, b, precision=None):
    return lax.dot_general(
        a, b, (((1,), (1,)), ((), ())), precision=precision, preferred_element_type=f32
    )


def normalize(rows):
    wide = rows.astype(f32)
    scale = lax.rsqrt(jnp.mean(wide * wide, axis=-1, keepdims=True) + eps_value)
    return (wide * scale).astype(bf16)


def bias_of(rows):
    wide = rows.astype(f32)
    width = rows.shape[1]
    return (width - jnp.sum(wide * wide, axis=1, keepdims=True)) / (2.0 * math.sqrt(width))


def as_row(column):
    return jnp.broadcast_to(column, (column.shape[0], 128)).T[0:1, :]


def kernel_tile(left, left_bias, right, right_bias_row):
    cross = dot_nt(left, right)
    return jnp.exp(cross * (1.0 / math.sqrt(left.shape[1])) + (left_bias + right_bias_row))


def augmented(labels):
    rows = labels.shape[0]
    turned = labels.astype(f32).T
    ones = (lax.broadcasted_iota(jnp.int32, (aug - labels.shape[1], rows), 0) == 0).astype(f32)
    return jnp.concatenate([turned, ones], axis=0).astype(bf16)


def whole(parts):
    last = parts.shape[0] - 1
    return jnp.concatenate(
        [parts[j, :step_rows] for j in range(last)] + [parts[last]], axis=0
    )


def kernel(
    n,
    docs_hbm,
    labels_hbm,
    skel_hbm,
    transfer_hbm,
    near_peer_hbm,
    near_live_hbm,
    couple_peer_hbm,
    couple_live_hbm,
    out_ref,
    docs_in,
    labels_in,
    skel_in,
    transfer_in,
    near_peer,
    near_live,
    couple_peer,
    couple_live,
    docs,
    docs_bias,
    docs_row,
    lab_t,
    pts,
    leaf,
    docs_r,
    labels_r,
    lab_tr,
    p8,
    p2,
    p1,
    near_t,
    before_t,
    w0_send,
    w0_recv,
    t1_sum,
    t1_send,
    t1_recv,
    w1_parts,
    w1_own,
    w1_next,
    t2_send,
    t2_recv,
    w2_parts,
    w2_next,
    w2_pair,
    ret0_send,
    ret0_recv,
    ret1_send,
    ret1_recv,
    ret2_send,
    ret2_recv,
    near_send,
    near_recv,
    in_sem,
    send_sem,
    recv_sem,
):
    me = lax.axis_index("doc")
    count = docs_in.shape[0]
    rank = skel_in.shape[0]
    pieces = count // chunk
    core = lax.rem(me, 2)
    quarter = lax.rem(me, 4)

    def piece(i):
        return pl.ds(pl.multiple_of(i * chunk, chunk), chunk)

    def part_rows(j):
        return pl.ds(pl.multiple_of(j * step_rows, step_rows), part)

    def fetch(slot, src, dst):
        return pltpu.make_async_copy(src, dst, in_sem.at[slot])

    def docs_fetch(i):
        return fetch(IN_DOCS + i, docs_hbm.at[piece(i)], docs_in.at[piece(i)])

    f_skel = fetch(IN_SKEL, skel_hbm, skel_in)
    f_skel.start()
    for i in range(pieces):
        docs_fetch(i).start()
    f_labels = fetch(IN_LABELS, labels_hbm, labels_in)
    f_labels.start()
    f_transfer = fetch(IN_TRANSFER, transfer_hbm, transfer_in)
    f_transfer.start()
    f_lists = [
        fetch(IN_LISTS, near_peer_hbm, near_peer),
        fetch(IN_LISTS + 1, near_live_hbm, near_live),
        fetch(IN_LISTS + 2, couple_peer_hbm, couple_peer),
        fetch(IN_LISTS + 3, couple_live_hbm, couple_live),
    ]
    for f in f_lists:
        f.start()

    def at(offset):
        return lax.rem(me + offset + n, n)

    def flipped(place, bits):
        low = lax.rem(place, 2)
        high = lax.rem(place // 2, 2)
        return (1 - 2 * low) * (bits % 2) + (2 - 4 * high) * (bits // 2)

    def sibling(bits, unit):
        return me + flipped(me // unit, bits) * unit

    def inside(offset):
        return jnp.logical_and(me + offset >= 0, me + offset < n)

    class Flow:
        def __init__(self, flow, src, dst, target, out=None, into=None):
            self.copy = pltpu.make_async_remote_copy(
                src_ref=src,
                dst_ref=dst,
                send_sem=send_sem.at[flow],
                recv_sem=recv_sem.at[flow],
                device_id=(target,),
                device_id_type=MESH,
            )
            self.out = out
            self.into = into

        def start(self):
            when(self.out, self.copy.start)
            return self

        def wait_recv(self):
            when(self.into, self.copy.wait_recv)

        def wait_send(self):
            when(self.out, self.copy.wait_send)

    def when(condition, action):
        if condition is None:
            action()
        else:
            pl.when(condition)(lambda: action() and None)

    def along(flow, src, dst, offset, out=True, into=True):
        return Flow(
            flow,
            src,
            dst,
            at(offset),
            inside(offset) if out is True else jnp.logical_and(inside(offset), out),
            inside(-offset) if into is True else jnp.logical_and(inside(-offset), into),
        )

    def send(flow, src, dst, target, out=None, into=None):
        return Flow(flow, src, dst, target, out, into).start()

    even = core == 0
    odd = core == 1
    next1 = jnp.where(even, jnp.where(quarter < 2, at(-2), at(2)), at(-4))
    low1 = jnp.logical_and(even, quarter < 2)

    out1 = jnp.where(even, jnp.where(quarter < 2, me >= 2, me + 2 < n), me >= 4)
    into1 = jnp.where(even, out1, me + 4 < n)

    spot = lax.rem(me // 2, 16)
    base = me - lax.rem(me, 32)
    up4 = base + lax.rem(spot + 4, 16) * 2 + core
    down4 = base + lax.rem(spot + 12, 16) * 2 + core
    half = spot // 8
    central = jnp.logical_and(spot >= 4, spot < 12)
    meet = central == even
    first_half = half == 0
    meeting = jnp.where(first_half == even, up4, down4)
    from_a = jnp.where(even, down4, up4)
    from_b = jnp.where(even, up4, down4)
    other_half = jnp.where(central == first_half, up4, down4)
    has_next = me < n - 32
    has_last = me >= 32
    meet_next = jnp.logical_and(meet, has_next)
    meet_last = jnp.logical_and(meet, has_last)
    b_next = jnp.logical_and(half == 1, has_next)
    a_last = jnp.logical_and(first_half, has_last)

    barrier = pltpu.get_barrier_semaphore()
    reach = (1, 2, 4, 32)
    for other in [sibling(3, 1), sibling(3, 4), up4, down4]:
        pl.semaphore_signal(barrier, inc=1, device_id=(other,), device_id_type=MESH)
    for offset in [sign * far for far in reach for sign in (1, -1)]:

        @pl.when(inside(offset))
        def _(offset=offset):
            pl.semaphore_signal(barrier, inc=1, device_id=(at(offset),), device_id_type=MESH)

    @pl.when(b_next)
    def _():
        pl.semaphore_signal(barrier, inc=1, device_id=(meeting + 32,), device_id_type=MESH)

    @pl.when(jnp.logical_and(first_half, jnp.logical_not(has_last)))
    def _():
        ret2_recv[1] = jnp.zeros_like(ret2_recv[1])

    @pl.when(jnp.logical_and(half == 1, jnp.logical_not(has_next)))
    def _():
        ret2_recv[0] = jnp.zeros_like(ret2_recv[0])

    @pl.when(me < 4)
    def _():
        p2[0] = jnp.zeros_like(p2[0])
        ret1_recv[1] = jnp.zeros_like(ret1_recv[1])

    @pl.when(me >= n - 4)
    def _():
        p2[1] = jnp.zeros_like(p2[1])
        ret1_recv[0] = jnp.zeros_like(ret1_recv[0])

    @pl.when(jnp.logical_not(into1))
    def _():
        w1_next[...] = jnp.zeros_like(w1_next)

    @pl.when(me == 0)
    def _():
        docs_r[...] = jnp.zeros_like(docs_r)
        labels_r[...] = jnp.zeros_like(labels_r)
        ret0_recv[...] = jnp.zeros_like(ret0_recv)

    @pl.when(me == n - 1)
    def _():
        p1[...] = jnp.zeros_like(p1)
        w0_recv[...] = jnp.zeros_like(w0_recv)
        near_recv[...] = jnp.zeros_like(near_recv)

    f_skel.wait()
    pts[...] = normalize(skel_in[...])
    def strip_copy(slot, k):
        size = rank // strips
        rows = pl.ds(k * size, size)
        return Flow(
            PTS8 + slot * strips + k, pts.at[rows], p8.at[slot, rows], meeting, None, meet
        )

    def strip(k):
        strip_copy(half, k).start()


    def docs_copy(i):
        return along(DOCS + i, docs.at[piece(i)], docs_r.at[piece(i)], 1)

    def near_copy(i):
        return along(NEAR + i, near_send.at[i], near_recv.at[i], -1)

    @pl.loop(0, pieces)
    def _(i):
        docs_fetch(i).wait()
        docs[piece(i), :] = normalize(docs_in[piece(i), :])

    f_labels.wait()
    lab_t[...] = augmented(labels_in[...])
    pts_bias = bias_of(pts[...])
    pts_row = as_row(pts_bias)

    @pl.loop(0, pieces)
    def _(i):
        rows = piece(i)
        block = docs[rows, :]
        bias = bias_of(block)
        docs_bias[rows, :] = bias
        docs_row[:, rows] = as_row(bias)
        leaf[rows, :] = kernel_tile(block, bias, pts[...], pts_row).astype(bf16)

    w0 = dot_nn(lab_t[...], leaf[...]) * (1.0 / count)
    w0_send[...] = w0.astype(bf16)

    f_transfer.wait()
    child2 = lax.rem(me // 4, 4)
    t1 = 0.25 * dot_nn(w0, transfer_in[0, quarter], highest)
    t1_sum[...] = t1
    t1_send[...] = t1.astype(bf16)

    greetings = 4 + jnp.where(meet_last, 1, 0)
    for offset in [sign * far for far in reach for sign in (1, -1)]:
        greetings = greetings + jnp.where(inside(offset), 1, 0)
    pl.semaphore_wait(barrier, greetings)

    c_t1 = [
        send(
            T1 + j,
            t1_send.at[part_rows(quarter + flipped(quarter, j + 1))],
            t1_recv.at[j],
            sibling(j + 1, 1),
        )
        for j in range(3)
    ]

    c_w0 = along(W0, w0_send, w0_recv, -1).start()

    strip(0)

    near_t[...] = jnp.zeros_like(near_t)

    @pl.loop(0, pieces)
    def _(i):
        rows = piece(i)
        tile = kernel_tile(docs[rows, :], docs_bias[rows, :], docs[...], docs_row[...])
        row_ids = lax.broadcasted_iota(jnp.int32, tile.shape, 0) + i * chunk
        col_ids = lax.broadcasted_iota(jnp.int32, tile.shape, 1)
        tile = jnp.where(row_ids == col_ids, 0.0, tile).astype(bf16)
        near_t[...] += dot_nn(lab_t[:, rows], tile)

    for copy in c_t1:
        copy.wait_recv()
    w1 = (t1_sum[part_rows(quarter), :] + t1_recv[0].astype(f32)) + (
        t1_recv[1].astype(f32) + t1_recv[2].astype(f32)
    )
    w1_parts[quarter] = w1.astype(bf16)
    t2 = 0.25 * dot_nn(w1, transfer_in[1, child2], highest)
    t2_send[...] = t2.astype(bf16)
    c_t2 = [send(T2 + j, t2_send, t2_recv.at[j], sibling(j + 1, 4)) for j in range(3)]
    c_share1 = [
        send(SHARE1 + j, w1_parts.at[quarter], w1_parts.at[quarter], sibling(j + 1, 1))
        for j in range(3)
    ]
    strip(1)

    for copy in c_t2:
        copy.wait_recv()
    w2 = (t2 + t2_recv[0].astype(f32)) + (t2_recv[1].astype(f32) + t2_recv[2].astype(f32))
    w2_parts[quarter] = w2.astype(bf16)
    c_shift2 = send(SHIFT2, w2_parts.at[quarter], w2_next.at[quarter], other_half)
    c_share2 = [
        send(
            SHARE2 + j,
            w2_parts.at[quarter],
            w2_parts.at[quarter],
            sibling(j + 1, 1),
            meet if j == 1 else jnp.logical_not(meet),
            meet,
        )
        for j in range(3)
    ]

    for copy in c_share1:
        copy.wait_recv()
    w1_own[...] = whole(w1_parts)
    c_w1 = send(W1, w1_own, w1_next, next1, out1, into1)
    level1 = [
        along(PTS_DOWN, pts, p2.at[1], -2, even, even),
        along(PTS_DOWN, pts, p2.at[1], -4, odd, odd),
        along(PTS_UP2, pts, p2.at[0], 2, even, even),
    ]
    for copy in level1:
        copy.start()


    c_shift2.wait_recv()
    c_share_next = [
        send(
            SHARE_NEXT + j,
            w2_next.at[quarter],
            w2_next.at[quarter],
            sibling(j + 1, 1),
            meet if j == 1 else jnp.logical_not(meet),
            meet,
        )
        for j in range(3)
    ]


    for k in range(strips):
        strip_copy(1, k).wait_recv()
    c_forward = send(FORWARD, p8.at[1], p8.at[2], at(32), meet_next, meet_last)
    c_down1 = along(PTS_DOWN1, pts, p1, -1).start()
    c_labels = along(LABELS, labels_in, labels_r, 1).start()
    docs_copy(0).start()
    docs_copy(1).start()
    docs_copy(2).start()

    for copy in c_share2 + c_share_next:
        copy.wait_recv()

    @pl.when(meet)
    def _():
        own2 = whole(w2_parts)
        other2 = whole(w2_next)
        w2_pair[0] = jnp.where(first_half, own2, other2)
        w2_pair[1] = jnp.where(first_half, other2, own2)

    c_wforward = send(W_FORWARD, w2_pair.at[1], w2_pair.at[2], at(32), meet_next, meet_last)
    for k in range(strips):
        strip_copy(0, k).wait_recv()

    def couple2(left, right):
        return kernel_tile(
            left, bias_of(left), right, as_row(bias_of(right))
        ).astype(bf16)

    @pl.when(meet)
    def _():
        pair = couple2(p8[0], p8[1])
        ret2_send[0] = dot_nt(w2_pair[1], pair).astype(bf16)
        ret2_send[1] = dot_nn(w2_pair[0], pair).astype(bf16)

    def ret2(j, slot, target, out, into):
        return send(RET2 + j, ret2_send.at[j], ret2_recv.at[slot], target, out, into)

    c_ret2 = [
        ret2(0, 0, from_a, meet, first_half),
        ret2(1, 1, from_b, meet, half == 1),
    ]
    c_forward.wait_recv()
    c_wforward.wait_recv()

    @pl.when(meet_last)
    def _():
        pair = couple2(p8[2], p8[0])
        ret2_send[2] = dot_nt(w2_pair[0], pair).astype(bf16)
        ret2_send[3] = dot_nn(w2_pair[2], pair).astype(bf16)

    c_ret2 += [
        ret2(2, 0, from_b - 32, meet_last, b_next),
        ret2(3, 1, from_a, meet_last, a_last),
    ]

    c_down1.wait_recv()
    c_w0.wait_recv()
    pair = kernel_tile(pts[...], pts_bias, p1[...], as_row(bias_of(p1[...]))).astype(bf16)
    ret0_send[...] = dot_nn(w0_send[...], pair).astype(bf16)
    c_ret0 = along(RET0, ret0_send, ret0_recv, 1).start()
    after0 = dot_nt(w0_recv[...], pair)

    for copy in level1:
        copy.wait_recv()

    @pl.when(odd)
    def _():
        p2[0] = pts[...]

    c_w1.wait_recv()
    pair = kernel_tile(
        p2[0], bias_of(p2[0]), p2[1], as_row(bias_of(p2[1]))
    ).astype(bf16)
    w_before = jnp.where(low1, w1_next[...], w1_own[...])
    w_after = jnp.where(low1, w1_own[...], w1_next[...])
    ret1_send[0] = dot_nt(w_after, pair).astype(bf16)
    ret1_send[1] = dot_nn(w_before, pair).astype(bf16)
    c_ret1 = [
        along(RET1_UP, ret1_send.at[1], ret1_recv.at[1], 2, even, even).start(),
        along(RET1_UP, ret1_send.at[1], ret1_recv.at[1], 4, odd, odd).start(),
        along(RET1_DOWN, ret1_send.at[0], ret1_recv.at[0], -2, even, even).start(),
    ]

    @pl.when(odd)
    def _():
        ret1_recv[0] = ret1_send[0]

    c_labels.wait_recv()
    lab_tr[...] = augmented(labels_r[...])
    before_t[...] = jnp.zeros_like(before_t)

    @pl.loop(0, pieces)
    def _(i):
        rows = piece(i)
        docs_copy(i).wait_recv()
        block = docs_r[rows, :]
        tile = kernel_tile(block, bias_of(block), docs[...], docs_row[...]).astype(bf16)
        near_send[i] = dot_nt(lab_t[...], tile).astype(bf16)
        near_copy(i).start()
        before_t[...] += dot_nn(lab_tr[:, rows], tile)

    def tally(peer, live, code, inside):
        total = jnp.int32(0)
        for p, v in zip(peer, live):
            total = total + v * (p == code).astype(jnp.int32)
        return (total * inside.astype(jnp.int32)).astype(f32)

    def tallies(peer, live, stride):
        return (
            tally(peer, live, 0, me >= stride),
            tally(peer, live, 1, me <= n - 1 - stride),
        )

    for f in f_lists:
        f.wait()
    slots = near_peer.shape[1]
    near_before, near_after = tallies(
        [near_peer[0, j] for j in range(slots)], [near_live[0, j] for j in range(slots)], 1
    )
    couple = [
        tallies(
            [couple_peer[0, j, level] for j in range(slots)],
            [couple_live[0, j, level] for j in range(slots)],
            4**level,
        )
        for level in range(3)
    ]

    c_ret0.wait_recv()
    far0 = (couple[0][0] * ret0_recv[...].astype(f32) + couple[0][1] * after0) / rank
    for copy in c_ret1:
        copy.wait_recv()

    far1 = (
        couple[1][1] * ret1_recv[0].astype(f32) + couple[1][0] * ret1_recv[1].astype(f32)
    ) / rank

    for copy in c_ret2:
        copy.wait_recv()
    down = (
        couple[2][1] * ret2_recv[0].astype(f32) + couple[2][0] * ret2_recv[1].astype(f32)
    ) / rank
    down = far1 + dot_nt(down, transfer_in[1, child2], highest)
    down = far0 + dot_nt(down, transfer_in[0, quarter], highest)
    down_high = down.astype(bf16)
    down_low = (down - down_high.astype(f32)).astype(bf16)
    far = dot_nt(down_high, leaf[...]) + dot_nt(down_low, leaf[...])

    @pl.loop(0, pieces)
    def _(i):
        rows = piece(i)
        near_copy(i).wait_recv()
        near_t[:, rows] += (
            near_before * before_t[:, rows] + near_after * near_recv[i].astype(f32)
        )

    total = near_t[...] + (far_gain / rank) * far
    width = labels_in.shape[1]
    out_ref[...] = (total[:width] / total[width : width + 1]).T

    for copies in (
        [c_down1, c_labels, c_w0, c_w1, c_shift2, c_ret0],
        c_t1 + c_share1 + c_t2 + c_share2 + c_share_next,
        level1 + c_ret1 + c_ret2,
        [c_forward, c_wforward] + [strip_copy(half, k) for k in range(strips)],
    ):
        for copy in copies:
            copy.wait_send()

    @pl.loop(0, pieces)
    def _(i):
        docs_copy(i).wait_send()
        near_copy(i).wait_send()


def solution(mesh):
    n = mesh.shape["doc"]

    def local(documents, labels, skeleton, transfer, near_peer, near_live, couple_peer, couple_live):
        count, depth = documents.shape
        width = labels.shape[1]
        rank = skeleton.shape[0]
        pieces = count // chunk
        node = lambda *lead: pltpu.VMEM((*lead, aug, rank), bf16)
        parts = lambda lead: pltpu.VMEM((lead, part, rank), bf16)
        anywhere = pl.BlockSpec(memory_space=pl.ANY)
        couple_peer = couple_peer.transpose(0, 2, 1)
        couple_live = couple_live.transpose(0, 2, 1)
        return pl.pallas_call(
            functools.partial(kernel, n),
            out_shape=jax.ShapeDtypeStruct((count, width), f32),
            in_specs=[anywhere] * 8,
            out_specs=pl.BlockSpec(memory_space=pltpu.VMEM),
            scratch_shapes=[
                pltpu.VMEM((count, depth), bf16),
                pltpu.VMEM((count, width), bf16),
                pltpu.VMEM((rank, depth), bf16),
                pltpu.VMEM(transfer.shape, f32),
                pltpu.SMEM(near_peer.shape, jnp.int32),
                pltpu.SMEM(near_live.shape, jnp.int32),
                pltpu.SMEM(couple_peer.shape, jnp.int32),
                pltpu.SMEM(couple_live.shape, jnp.int32),
                pltpu.VMEM((count, depth), bf16),
                pltpu.VMEM((count, 1), f32),
                pltpu.VMEM((1, count), f32),
                pltpu.VMEM((aug, count), bf16),
                pltpu.VMEM((rank, depth), bf16),
                pltpu.VMEM((count, rank), bf16),
                pltpu.VMEM((count, depth), bf16),
                pltpu.VMEM((count, width), bf16),
                pltpu.VMEM((aug, count), bf16),
                pltpu.VMEM((3, rank, depth), bf16),
                pltpu.VMEM((2, rank, depth), bf16),
                pltpu.VMEM((rank, depth), bf16),
                pltpu.VMEM((aug, count), f32),
                pltpu.VMEM((aug, count), f32),
                node(),
                node(),
                pltpu.VMEM((aug, rank), f32),
                node(),
                parts(3),
                parts(4),
                node(),
                node(),
                pltpu.VMEM((part, rank), bf16),
                parts(3),
                parts(4),
                parts(4),
                node(3),
                node(),
                node(),
                node(2),
                node(2),
                node(4),
                node(2),
                node(pieces),
                node(pieces),
                pltpu.SemaphoreType.DMA((INPUTS,)),
                pltpu.SemaphoreType.DMA((FLOWS,)),
                pltpu.SemaphoreType.DMA((FLOWS,)),
            ],
            compiler_params=pltpu.CompilerParams(
                collective_id=0, has_side_effects=True, vmem_limit_bytes=60 * 2**20
            ),
        )(documents, labels, skeleton, transfer, near_peer, near_live, couple_peer, couple_live)

    placed = (
        P("doc", None),
        P("doc", None),
        P("doc", None),
        P(),
        P("doc", None),
        P("doc", None),
        P("doc", None, None),
        P("doc", None, None),
    )
    return jax.shard_map(
        local, mesh=mesh, in_specs=placed, out_specs=P("doc", None), check_vma=False
    )
```

```python
import functools
import math

import jax
import jax.numpy as jnp
from jax import lax
from jax.experimental import pallas as pl
from jax.experimental.pallas import tpu as pltpu
from jax.sharding import PartitionSpec as P

MESH = pl.DeviceIdType.MESH
f32 = jnp.float32
bf16 = jnp.bfloat16
highest = lax.Precision.HIGHEST
eps_value = 1e-06
far_gain = 64.0
chunk = 256
aug = 144

PTS_UP2, PTS_DOWN, PTS_DOWN1 = range(3)
DOCS = 5
LABELS = 8
W0 = 9
T1 = 10
SHARE1 = 13
W1 = 16
T2 = 17
SHARE2 = 20
SHIFT2 = 23
SHARE_NEXT = 24
RET0 = 27
RET1_DOWN, RET1_UP = 28, 29
NEAR = 30
PTS8 = 33
FORWARD, W_FORWARD = 37, 38
RET2 = 39
FLOWS = 43

strips = 2

part = 48
step_rows = 32

IN_SKEL = 0
IN_LABELS = 1
IN_TRANSFER = 2
IN_LISTS = 3
IN_DOCS = 7
INPUTS = 10


def dot_nn(a, b, precision=None):
    return lax.dot_general(
        a, b, (((1,), (0,)), ((), ())), precision=precision, preferred_element_type=f32
    )


def dot_nt(a, b, precision=None):
    return lax.dot_general(
        a, b, (((1,), (1,)), ((), ())), precision=precision, preferred_element_type=f32
    )


def normalize(rows):
    wide = rows.astype(f32)
    scale = lax.rsqrt(jnp.mean(wide * wide, axis=-1, keepdims=True) + eps_value)
    return (wide * scale).astype(bf16)


def bias_of(rows):
    wide = rows.astype(f32)
    width = rows.shape[1]
    return (width - jnp.sum(wide * wide, axis=1, keepdims=True)) / (2.0 * math.sqrt(width))


def as_row(column):
    return jnp.broadcast_to(column, (column.shape[0], 128)).T[0:1, :]


def kernel_tile(left, left_bias, right, right_bias_row):
    cross = dot_nt(left, right)
    return jnp.exp(cross * (1.0 / math.sqrt(left.shape[1])) + (left_bias + right_bias_row))


def augmented(labels):
    rows = labels.shape[0]
    turned = labels.astype(f32).T
    ones = (lax.broadcasted_iota(jnp.int32, (aug - labels.shape[1], rows), 0) == 0).astype(f32)
    return jnp.concatenate([turned, ones], axis=0).astype(bf16)


def whole(parts):
    last = parts.shape[0] - 1
    return jnp.concatenate(
        [parts[j, :step_rows] for j in range(last)] + [parts[last]], axis=0
    )


def kernel(
    n,
    docs_hbm,
    labels_hbm,
    skel_hbm,
    transfer_hbm,
    near_peer_hbm,
    near_live_hbm,
    couple_peer_hbm,
    couple_live_hbm,
    out_ref,
    docs_in,
    labels_in,
    skel_in,
    transfer_in,
    near_peer,
    near_live,
    couple_peer,
    couple_live,
    docs,
    docs_bias,
    docs_row,
    lab_t,
    pts,
    leaf,
    docs_r,
    labels_r,
    lab_tr,
    p8,
    p2,
    p1,
    near_t,
    before_t,
    w0_send,
    w0_recv,
    t1_sum,
    t1_send,
    t1_recv,
    w1_parts,
    w1_own,
    w1_next,
    t2_send,
    t2_recv,
    w2_parts,
    w2_next,
    w2_pair,
    ret0_send,
    ret0_recv,
    ret1_send,
    ret1_recv,
    ret2_send,
    ret2_recv,
    near_send,
    near_recv,
    in_sem,
    send_sem,
    recv_sem,
):
    me = lax.axis_index("doc")
    count = docs_in.shape[0]
    rank = skel_in.shape[0]
    pieces = count // chunk
    core = lax.rem(me, 2)
    quarter = lax.rem(me, 4)

    def piece(i):
        return pl.ds(pl.multiple_of(i * chunk, chunk), chunk)

    def part_rows(j):
        return pl.ds(pl.multiple_of(j * step_rows, step_rows), part)

    def fetch(slot, src, dst):
        return pltpu.make_async_copy(src, dst, in_sem.at[slot])

    def docs_fetch(i):
        return fetch(IN_DOCS + i, docs_hbm.at[piece(i)], docs_in.at[piece(i)])

    f_skel = fetch(IN_SKEL, skel_hbm, skel_in)
    f_skel.start()
    for i in range(pieces):
        docs_fetch(i).start()
    f_labels = fetch(IN_LABELS, labels_hbm, labels_in)
    f_labels.start()
    f_transfer = fetch(IN_TRANSFER, transfer_hbm, transfer_in)
    f_transfer.start()
    f_lists = [
        fetch(IN_LISTS, near_peer_hbm, near_peer),
        fetch(IN_LISTS + 1, near_live_hbm, near_live),
        fetch(IN_LISTS + 2, couple_peer_hbm, couple_peer),
        fetch(IN_LISTS + 3, couple_live_hbm, couple_live),
    ]
    for f in f_lists:
        f.start()

    def at(offset):
        return lax.rem(me + offset + n, n)

    def flipped(place, bits):
        low = lax.rem(place, 2)
        high = lax.rem(place // 2, 2)
        return (1 - 2 * low) * (bits % 2) + (2 - 4 * high) * (bits // 2)

    def sibling(bits, unit):
        return me + flipped(me // unit, bits) * unit

    def inside(offset):
        return jnp.logical_and(me + offset >= 0, me + offset < n)

    class Flow:
        def __init__(self, flow, src, dst, target, out=None, into=None):
            self.copy = pltpu.make_async_remote_copy(
                src_ref=src,
                dst_ref=dst,
                send_sem=send_sem.at[flow],
                recv_sem=recv_sem.at[flow],
                device_id=(target,),
                device_id_type=MESH,
            )
            self.out = out
            self.into = into

        def start(self):
            when(self.out, self.copy.start)
            return self

        def wait_recv(self):
            when(self.into, self.copy.wait_recv)

        def wait_send(self):
            when(self.out, self.copy.wait_send)

    def when(condition, action):
        if condition is None:
            action()
        else:
            pl.when(condition)(lambda: action() and None)

    def along(flow, src, dst, offset, out=True, into=True):
        return Flow(
            flow,
            src,
            dst,
            at(offset),
            inside(offset) if out is True else jnp.logical_and(inside(offset), out),
            inside(-offset) if into is True else jnp.logical_and(inside(-offset), into),
        )

    def send(flow, src, dst, target, out=None, into=None):
        return Flow(flow, src, dst, target, out, into).start()

    even = core == 0
    odd = core == 1
    next1 = jnp.where(even, jnp.where(quarter < 2, at(-2), at(2)), at(-4))
    low1 = jnp.logical_and(even, quarter < 2)

    out1 = jnp.where(even, jnp.where(quarter < 2, me >= 2, me + 2 < n), me >= 4)
    into1 = jnp.where(even, out1, me + 4 < n)

    spot = lax.rem(me // 2, 16)
    base = me - lax.rem(me, 32)
    up4 = base + lax.rem(spot + 4, 16) * 2 + core
    down4 = base + lax.rem(spot + 12, 16) * 2 + core
    half = spot // 8
    central = jnp.logical_and(spot >= 4, spot < 12)
    meet = central == even
    first_half = half == 0
    meeting = jnp.where(first_half == even, up4, down4)
    from_a = jnp.where(even, down4, up4)
    from_b = jnp.where(even, up4, down4)
    other_half = jnp.where(central == first_half, up4, down4)
    has_next = me < n - 32
    has_last = me >= 32
    meet_next = jnp.logical_and(meet, has_next)
    meet_last = jnp.logical_and(meet, has_last)
    b_next = jnp.logical_and(half == 1, has_next)
    a_last = jnp.logical_and(first_half, has_last)

    barrier = pltpu.get_barrier_semaphore()
    reach = (1, 2, 4, 32)
    for other in [sibling(3, 1), sibling(3, 4), up4, down4]:
        pl.semaphore_signal(barrier, inc=1, device_id=(other,), device_id_type=MESH)
    for offset in [sign * far for far in reach for sign in (1, -1)]:

        @pl.when(inside(offset))
        def _(offset=offset):
            pl.semaphore_signal(barrier, inc=1, device_id=(at(offset),), device_id_type=MESH)

    @pl.when(b_next)
    def _():
        pl.semaphore_signal(barrier, inc=1, device_id=(meeting + 32,), device_id_type=MESH)

    @pl.when(jnp.logical_and(first_half, jnp.logical_not(has_last)))
    def _():
        ret2_recv[1] = jnp.zeros_like(ret2_recv[1])

    @pl.when(jnp.logical_and(half == 1, jnp.logical_not(has_next)))
    def _():
        ret2_recv[0] = jnp.zeros_like(ret2_recv[0])

    @pl.when(me < 4)
    def _():
        p2[0] = jnp.zeros_like(p2[0])
        ret1_recv[1] = jnp.zeros_like(ret1_recv[1])

    @pl.when(me >= n - 4)
    def _():
        p2[1] = jnp.zeros_like(p2[1])
        ret1_recv[0] = jnp.zeros_like(ret1_recv[0])

    @pl.when(jnp.logical_not(into1))
    def _():
        w1_next[...] = jnp.zeros_like(w1_next)

    @pl.when(me == 0)
    def _():
        docs_r[...] = jnp.zeros_like(docs_r)
        labels_r[...] = jnp.zeros_like(labels_r)
        ret0_recv[...] = jnp.zeros_like(ret0_recv)

    @pl.when(me == n - 1)
    def _():
        p1[...] = jnp.zeros_like(p1)
        w0_recv[...] = jnp.zeros_like(w0_recv)
        near_recv[...] = jnp.zeros_like(near_recv)

    f_skel.wait()
    pts[...] = normalize(skel_in[...])
    def strip_copy(slot, k):
        size = rank // strips
        rows = pl.ds(k * size, size)
        return Flow(
            PTS8 + slot * strips + k, pts.at[rows], p8.at[slot, rows], meeting, None, meet
        )

    def strip(k):
        strip_copy(half, k).start()


    def docs_copy(i):
        return along(DOCS + i, docs.at[piece(i)], docs_r.at[piece(i)], 1)

    def near_copy(i):
        return along(NEAR + i, near_send.at[i], near_recv.at[i], -1)

    @pl.loop(0, pieces)
    def _(i):
        docs_fetch(i).wait()
        docs[piece(i), :] = normalize(docs_in[piece(i), :])

    f_labels.wait()
    lab_t[...] = augmented(labels_in[...])
    pts_bias = bias_of(pts[...])
    pts_row = as_row(pts_bias)

    @pl.loop(0, pieces)
    def _(i):
        rows = piece(i)
        block = docs[rows, :]
        bias = bias_of(block)
        docs_bias[rows, :] = bias
        docs_row[:, rows] = as_row(bias)
        leaf[rows, :] = kernel_tile(block, bias, pts[...], pts_row).astype(bf16)

    w0 = dot_nn(lab_t[...], leaf[...]) * (1.0 / count)
    w0_send[...] = w0.astype(bf16)

    f_transfer.wait()
    child2 = lax.rem(me // 4, 4)
    t1 = 0.25 * dot_nn(w0, transfer_in[0, quarter], highest)
    t1_sum[...] = t1
    t1_send[...] = t1.astype(bf16)

    greetings = 4 + jnp.where(meet_last, 1, 0)
    for offset in [sign * far for far in reach for sign in (1, -1)]:
        greetings = greetings + jnp.where(inside(offset), 1, 0)
    pl.semaphore_wait(barrier, greetings)

    c_t1 = [
        send(
            T1 + j,
            t1_send.at[part_rows(quarter + flipped(quarter, j + 1))],
            t1_recv.at[j],
            sibling(j + 1, 1),
        )
        for j in range(3)
    ]

    c_w0 = along(W0, w0_send, w0_recv, -1).start()

    strip(0)

    near_t[...] = jnp.zeros_like(near_t)

    @pl.loop(0, pieces)
    def _(i):
        rows = piece(i)
        tile = kernel_tile(docs[rows, :], docs_bias[rows, :], docs[...], docs_row[...])
        row_ids = lax.broadcasted_iota(jnp.int32, tile.shape, 0) + i * chunk
        col_ids = lax.broadcasted_iota(jnp.int32, tile.shape, 1)
        tile = jnp.where(row_ids == col_ids, 0.0, tile).astype(bf16)
        near_t[...] += dot_nn(lab_t[:, rows], tile)

    for copy in c_t1:
        copy.wait_recv()
    w1 = (t1_sum[part_rows(quarter), :] + t1_recv[0].astype(f32)) + (
        t1_recv[1].astype(f32) + t1_recv[2].astype(f32)
    )
    w1_parts[quarter] = w1.astype(bf16)
    t2 = 0.25 * dot_nn(w1, transfer_in[1, child2], highest)
    t2_send[...] = t2.astype(bf16)
    c_t2 = [send(T2 + j, t2_send, t2_recv.at[j], sibling(j + 1, 4)) for j in range(3)]
    c_share1 = [
        send(SHARE1 + j, w1_parts.at[quarter], w1_parts.at[quarter], sibling(j + 1, 1))
        for j in range(3)
    ]
    strip(1)

    for copy in c_t2:
        copy.wait_recv()
    w2 = (t2 + t2_recv[0].astype(f32)) + (t2_recv[1].astype(f32) + t2_recv[2].astype(f32))
    w2_parts[quarter] = w2.astype(bf16)
    c_shift2 = send(SHIFT2, w2_parts.at[quarter], w2_next.at[quarter], other_half)
    c_share2 = [
        send(
            SHARE2 + j,
            w2_parts.at[quarter],
            w2_parts.at[quarter],
            sibling(j + 1, 1),
            meet if j == 1 else jnp.logical_not(meet),
            meet,
        )
        for j in range(3)
    ]

    for copy in c_share1:
        copy.wait_recv()
    w1_own[...] = whole(w1_parts)
    c_w1 = send(W1, w1_own, w1_next, next1, out1, into1)
    level1 = [
        along(PTS_DOWN, pts, p2.at[1], -2, even, even),
        along(PTS_DOWN, pts, p2.at[1], -4, odd, odd),
        along(PTS_UP2, pts, p2.at[0], 2, even, even),
    ]
    for copy in level1:
        copy.start()


    c_shift2.wait_recv()
    c_share_next = [
        send(
            SHARE_NEXT + j,
            w2_next.at[quarter],
            w2_next.at[quarter],
            sibling(j + 1, 1),
            meet if j == 1 else jnp.logical_not(meet),
            meet,
        )
        for j in range(3)
    ]


    for k in range(strips):
        strip_copy(1, k).wait_recv()
    c_forward = send(FORWARD, p8.at[1], p8.at[2], at(32), meet_next, meet_last)
    c_down1 = along(PTS_DOWN1, pts, p1, -1).start()
    c_labels = along(LABELS, labels_in, labels_r, 1).start()
    docs_copy(0).start()
    docs_copy(1).start()
    docs_copy(2).start()

    for copy in c_share2 + c_share_next:
        copy.wait_recv()

    @pl.when(meet)
    def _():
        own2 = whole(w2_parts)
        other2 = whole(w2_next)
        w2_pair[0] = jnp.where(first_half, own2, other2)
        w2_pair[1] = jnp.where(first_half, other2, own2)

    c_wforward = send(W_FORWARD, w2_pair.at[1], w2_pair.at[2], at(32), meet_next, meet_last)
    for k in range(strips):
        strip_copy(0, k).wait_recv()

    def couple2(left, right):
        return kernel_tile(
            left, bias_of(left), right, as_row(bias_of(right))
        ).astype(bf16)

    @pl.when(meet)
    def _():
        pair = couple2(p8[0], p8[1])
        ret2_send[0] = dot_nt(w2_pair[1], pair).astype(bf16)
        ret2_send[1] = dot_nn(w2_pair[0], pair).astype(bf16)

    def ret2(j, slot, target, out, into):
        return send(RET2 + j, ret2_send.at[j], ret2_recv.at[slot], target, out, into)

    c_ret2 = [
        ret2(0, 0, from_a, meet, first_half),
        ret2(1, 1, from_b, meet, half == 1),
    ]
    c_forward.wait_recv()
    c_wforward.wait_recv()

    @pl.when(meet_last)
    def _():
        pair = couple2(p8[2], p8[0])
        ret2_send[2] = dot_nt(w2_pair[0], pair).astype(bf16)
        ret2_send[3] = dot_nn(w2_pair[2], pair).astype(bf16)

    c_ret2 += [
        ret2(2, 0, from_b - 32, meet_last, b_next),
        ret2(3, 1, from_a, meet_last, a_last),
    ]

    c_down1.wait_recv()
    c_w0.wait_recv()
    pair = kernel_tile(pts[...], pts_bias, p1[...], as_row(bias_of(p1[...]))).astype(bf16)
    ret0_send[...] = dot_nn(w0_send[...], pair).astype(bf16)
    c_ret0 = along(RET0, ret0_send, ret0_recv, 1).start()
    after0 = dot_nt(w0_recv[...], pair)

    for copy in level1:
        copy.wait_recv()

    @pl.when(odd)
    def _():
        p2[0] = pts[...]

    c_w1.wait_recv()
    pair = kernel_tile(
        p2[0], bias_of(p2[0]), p2[1], as_row(bias_of(p2[1]))
    ).astype(bf16)
    w_before = jnp.where(low1, w1_next[...], w1_own[...])
    w_after = jnp.where(low1, w1_own[...], w1_next[...])
    ret1_send[0] = dot_nt(w_after, pair).astype(bf16)
    ret1_send[1] = dot_nn(w_before, pair).astype(bf16)
    c_ret1 = [
        along(RET1_UP, ret1_send.at[1], ret1_recv.at[1], 2, even, even).start(),
        along(RET1_UP, ret1_send.at[1], ret1_recv.at[1], 4, odd, odd).start(),
        along(RET1_DOWN, ret1_send.at[0], ret1_recv.at[0], -2, even, even).start(),
    ]

    @pl.when(odd)
    def _():
        ret1_recv[0] = ret1_send[0]

    c_labels.wait_recv()
    lab_tr[...] = augmented(labels_r[...])
    before_t[...] = jnp.zeros_like(before_t)

    @pl.loop(0, pieces)
    def _(i):
        rows = piece(i)
        docs_copy(i).wait_recv()
        block = docs_r[rows, :]
        tile = kernel_tile(block, bias_of(block), docs[...], docs_row[...]).astype(bf16)
        near_send[i] = dot_nt(lab_t[...], tile).astype(bf16)
        near_copy(i).start()
        before_t[...] += dot_nn(lab_tr[:, rows], tile)

    def tally(peer, live, code, inside):
        total = jnp.int32(0)
        for p, v in zip(peer, live):
            total = total + v * (p == code).astype(jnp.int32)
        return (total * inside.astype(jnp.int32)).astype(f32)

    def tallies(peer, live, stride):
        return (
            tally(peer, live, 0, me >= stride),
            tally(peer, live, 1, me <= n - 1 - stride),
        )

    for f in f_lists:
        f.wait()
    slots = near_peer.shape[1]
    near_before, near_after = tallies(
        [near_peer[0, j] for j in range(slots)], [near_live[0, j] for j in range(slots)], 1
    )
    couple = [
        tallies(
            [couple_peer[0, j, level] for j in range(slots)],
            [couple_live[0, j, level] for j in range(slots)],
            4**level,
        )
        for level in range(3)
    ]

    c_ret0.wait_recv()
    far0 = (couple[0][0] * ret0_recv[...].astype(f32) + couple[0][1] * after0) / rank
    for copy in c_ret1:
        copy.wait_recv()

    far1 = (
        couple[1][1] * ret1_recv[0].astype(f32) + couple[1][0] * ret1_recv[1].astype(f32)
    ) / rank

    for copy in c_ret2:
        copy.wait_recv()
    down = (
        couple[2][1] * ret2_recv[0].astype(f32) + couple[2][0] * ret2_recv[1].astype(f32)
    ) / rank
    down = far1 + dot_nt(down, transfer_in[1, child2], highest)
    down = far0 + dot_nt(down, transfer_in[0, quarter], highest)
    down_high = down.astype(bf16)
    down_low = (down - down_high.astype(f32)).astype(bf16)
    far = dot_nt(down_high, leaf[...]) + dot_nt(down_low, leaf[...])

    near_t[...] += near_before * before_t[...] + (far_gain / rank) * far
    width = labels_in.shape[1]

    @pl.loop(0, pieces)
    def _(i):
        rows = piece(i)
        near_copy(i).wait_recv()
        total = near_t[:, rows] + near_after * near_recv[i].astype(f32)
        out_ref[rows, :] = (total[:width] / total[width : width + 1]).T

    for copies in (
        [c_down1, c_labels, c_w0, c_w1, c_shift2, c_ret0],
        c_t1 + c_share1 + c_t2 + c_share2 + c_share_next,
        level1 + c_ret1 + c_ret2,
        [c_forward, c_wforward] + [strip_copy(half, k) for k in range(strips)],
    ):
        for copy in copies:
            copy.wait_send()

    @pl.loop(0, pieces)
    def _(i):
        docs_copy(i).wait_send()
        near_copy(i).wait_send()


def solution(mesh):
    n = mesh.shape["doc"]

    def local(documents, labels, skeleton, transfer, near_peer, near_live, couple_peer, couple_live):
        count, depth = documents.shape
        width = labels.shape[1]
        rank = skeleton.shape[0]
        pieces = count // chunk
        node = lambda *lead: pltpu.VMEM((*lead, aug, rank), bf16)
        parts = lambda lead: pltpu.VMEM((lead, part, rank), bf16)
        anywhere = pl.BlockSpec(memory_space=pl.ANY)
        couple_peer = couple_peer.transpose(0, 2, 1)
        couple_live = couple_live.transpose(0, 2, 1)
        return pl.pallas_call(
            functools.partial(kernel, n),
            out_shape=jax.ShapeDtypeStruct((count, width), f32),
            in_specs=[anywhere] * 8,
            out_specs=pl.BlockSpec(memory_space=pltpu.VMEM),
            scratch_shapes=[
                pltpu.VMEM((count, depth), bf16),
                pltpu.VMEM((count, width), bf16),
                pltpu.VMEM((rank, depth), bf16),
                pltpu.VMEM(transfer.shape, f32),
                pltpu.SMEM(near_peer.shape, jnp.int32),
                pltpu.SMEM(near_live.shape, jnp.int32),
                pltpu.SMEM(couple_peer.shape, jnp.int32),
                pltpu.SMEM(couple_live.shape, jnp.int32),
                pltpu.VMEM((count, depth), bf16),
                pltpu.VMEM((count, 1), f32),
                pltpu.VMEM((1, count), f32),
                pltpu.VMEM((aug, count), bf16),
                pltpu.VMEM((rank, depth), bf16),
                pltpu.VMEM((count, rank), bf16),
                pltpu.VMEM((count, depth), bf16),
                pltpu.VMEM((count, width), bf16),
                pltpu.VMEM((aug, count), bf16),
                pltpu.VMEM((3, rank, depth), bf16),
                pltpu.VMEM((2, rank, depth), bf16),
                pltpu.VMEM((rank, depth), bf16),
                pltpu.VMEM((aug, count), f32),
                pltpu.VMEM((aug, count), f32),
                node(),
                node(),
                pltpu.VMEM((aug, rank), f32),
                node(),
                parts(3),
                parts(4),
                node(),
                node(),
                pltpu.VMEM((part, rank), bf16),
                parts(3),
                parts(4),
                parts(4),
                node(3),
                node(),
                node(),
                node(2),
                node(2),
                node(4),
                node(2),
                node(pieces),
                node(pieces),
                pltpu.SemaphoreType.DMA((INPUTS,)),
                pltpu.SemaphoreType.DMA((FLOWS,)),
                pltpu.SemaphoreType.DMA((FLOWS,)),
            ],
            compiler_params=pltpu.CompilerParams(
                collective_id=0, has_side_effects=True, vmem_limit_bytes=60 * 2**20
            ),
        )(documents, labels, skeleton, transfer, near_peer, near_live, couple_peer, couple_live)

    placed = (
        P("doc", None),
        P("doc", None),
        P("doc", None),
        P(),
        P("doc", None),
        P("doc", None),
        P("doc", None, None),
        P("doc", None, None),
    )
    return jax.shard_map(
        local, mesh=mesh, in_specs=placed, out_specs=P("doc", None), check_vma=False
    )
```
